32 devices in a mesh: lat: 2 (over x), lon: 4 (over z), ch: 4 (over y, core).
Axes of the slice: x: 2, y: 2, z: 4, core: 2. Of those that a mesh axis runs over, the one named last changes fastest.
Arguments:
- features: bfloat16 [1, 14, 96, 1024], P(None, 'lat', 'lon', 'ch'), may hold values from -6 to 6
- kernel_one: bfloat16 [3, 3, 4, 256, 1024], P(None, None, 'ch', 'lon'), may hold values from -0.0625 to 0.0625
- bias_one: float32 [1024], P('ch'), may hold values from -3 to 3
- kernel_two: bfloat16 [3, 3, 4, 256, 1024], P(None, None, 'ch', 'lon'), may hold values from -0.0625 to 0.0625
- bias_two: float32 [1024], P('ch'), may hold values from -3 to 3
Outputs:
- outputs: bfloat16 [1, 14, 96, 1024], P(None, 'lat', 'lon', 'ch')
The draws below stay inside these ranges and needn't reach their ends.
All inputs are finite; a program needn't handle non-finite values.
Results may differ from the reference program's by a relative error of at most 0.01.
Values may be sent and summed in bfloat16 or wider, within the bound.
A program may use at most 64 MiB of HBM per device.

```python
import jax
import jax.numpy as jnp
from jax import lax

C = 1024
BATCH = 1
NLAT = 14
NLON = 96
N_CH = 4


def block_levels(own_key, shape, pieces, low, top_value):
    factor_of, own = 1.0, jax.random.fold_in(own_key, 6)
    for position, blocks in pieces:
        steps = jnp.exp(jax.random.uniform(jax.random.fold_in(own, position), (blocks,), jnp.float32, low / len(pieces), top_value / len(pieces)))
        factor_of = factor_of * jnp.repeat(steps, shape[position] // blocks).reshape([-1 if axis == position else 1 for axis in range(len(shape))])
    return factor_of


def normal_values(own_key, shape, deviation, bound, cuts=(), held_as=jnp.bfloat16):
    level = block_levels(own_key, shape, cuts, -0.22, 0.18) if cuts else 1.0
    entries = jax.random.normal(own_key, shape, jnp.float32) * deviation * level
    return jnp.minimum(jnp.maximum(entries, -bound), bound).astype(held_as)


def setup_inputs(seed: int = 0) -> dict:
    key_of = jax.random.split(jax.random.key(seed), 6)
    return {
        "features": normal_values(key_of[0], (BATCH, NLAT, NLON, C), 1.0, 6.0, ((1, 2), (2, 4), (3, 4))),
        "kernel_one": normal_values(key_of[1], (3, 3, N_CH, C // N_CH, C), (9 * C) ** -0.5, 0.0625, ((2, 4), (3, 4))),
        "bias_one": normal_values(key_of[2], (C,), 0.5, 3.0, ((0, 4),), jnp.float32),
        "kernel_two": normal_values(key_of[3], (3, 3, N_CH, C // N_CH, C), (9 * C) ** -0.5, 0.0625, ((2, 4), (3, 4))),
        "bias_two": normal_values(key_of[4], (C,), 0.5, 3.0, ((0, 4),), jnp.float32),
    }


skip_scale = 0.7071067811865476


def apply_taps(padded, kernel):
    count_items = padded.shape[0]
    height = padded.shape[1] - 2
    breadth = padded.shape[2] - 2
    channels = padded.shape[3]
    accumulated = jnp.zeros((count_items * height * breadth, kernel.shape[3]), jnp.float32)
    for row_off in range(3):
        for col_off in range(3):
            window = padded[:, row_off:row_off + height, col_off:col_off + breadth].reshape(-1, channels)
            accumulated = accumulated + jnp.dot(window, kernel[row_off, col_off], preferred_element_type=jnp.float32)
    return accumulated.reshape(count_items, height, breadth, kernel.shape[3])


def fold_pad(source):
    half_turn = source.shape[2] // 2
    top_row = jnp.roll(source[:, :1], half_turn, axis=2)
    low_row = jnp.roll(source[:, -1:], half_turn, axis=2)
    banded = jnp.concatenate([top_row, source, low_row], axis=1)
    return jnp.concatenate([banded[:, :, -1:], banded, banded[:, :, :1]], axis=2)


def conv_sum(activation, kernel_full, bias_vec):
    kernel = kernel_full.reshape(3, 3, C, C)
    padded = fold_pad(activation)
    width_group = C // N_CH

    def group_step(running, group_idx):
        start_idx = (group_idx * width_group).astype(jnp.int32)
        piece_in = lax.dynamic_slice_in_dim(padded, start_idx, width_group, 3)
        piece_kernel = lax.dynamic_slice_in_dim(kernel, start_idx, width_group, 2)
        partial_value = apply_taps(piece_in, piece_kernel).astype(jnp.bfloat16)
        partial_value = lax.optimization_barrier(partial_value)
        return running + partial_value.astype(jnp.float32), None

    initial = jnp.zeros(activation.shape[:3] + (C,), jnp.float32)
    summed, unused = lax.scan(group_step, initial, jnp.arange(N_CH, dtype=jnp.int32))
    return summed + bias_vec.astype(jnp.float32)


def reference(features, kernel_one, bias_one, kernel_two, bias_two):
    act_zero = jax.nn.silu(features.astype(jnp.float32)).astype(jnp.bfloat16)
    hidden = conv_sum(act_zero, kernel_one, bias_one)
    act_one = jax.nn.silu(hidden).astype(jnp.bfloat16)
    second = conv_sum(act_one, kernel_two, bias_two)
    return ((features.astype(jnp.float32) + second) * skip_scale).astype(jnp.bfloat16)
```

```python
import functools

import jax
import jax.numpy as jnp
from jax import lax
from jax.experimental import pallas as pl
from jax.experimental.pallas import tpu as pltpu
from jax.sharding import PartitionSpec as P

skip_scale = 0.7071067811865476
MESH = pl.DeviceIdType.MESH
EDGE = 8


def round_up(value, step):
    return -(-value // step) * step


def silu(value):
    return value / (1.0 + jnp.exp(-value))


def block_kernel(
    n_lat, n_lon, x_ref, k1_ref, b1_ref, k2_ref, b2_ref, out_ref,
    w, apack, arecv, hpack, hrecv, field, taps, acc, ysend, yrecv, zsend, zrecv,
    wl_sem, ws_sem, wr_sem, as_sem, ar_sem, hs_sem, hr_sem, ys_sem, yr_sem, zs_sem, zr_sem,
):
    rows, cols, width = x_ref.shape[1:]
    cells = rows * cols
    part = width // n_lon
    half = apack.shape[2]
    all_cols = cols * n_lon
    lat, lon, ch = lax.axis_index("lat"), lax.axis_index("lon"), lax.axis_index("ch")
    near = ch + 1 - 2 * (ch % 2)
    far = ch + 2 - 4 * ((ch // 2) % 2)
    near_far = near + 2 - 4 * ((near // 2) % 2)
    order = list(range(1, n_lon)) + [0]

    def device(up, along, channel):
        return {"lat": (lat + up) % n_lat, "lon": (lon + along) % n_lon, "ch": channel}

    def remote(src, dst, send, recv, target):
        return pltpu.make_async_remote_copy(
            src_ref=src, dst_ref=dst, send_sem=send, recv_sem=recv,
            device_id=target, device_id_type=MESH,
        )

    def weight_copies(conv, slot):
        source = (k1_ref, k2_ref)[conv]
        mine, theirs = ((ch, near), (far, near_far))[slot]

        def outputs(group):
            return source.at[:, :, 0, :, pl.ds(pl.multiple_of(group * width, width), width)]

        return (
            pltpu.make_async_copy(outputs(mine), w.at[conv, slot, :, :, 0], wl_sem.at[conv, slot]),
            remote(
                outputs(theirs), w.at[conv, slot, :, :, 1],
                ws_sem.at[conv, slot], wr_sem.at[conv, slot], device(0, 0, near),
            ),
        )

    weights = {(conv, slot): weight_copies(conv, slot) for conv in (0, 1) for slot in (1, 0)}
    for local, _ in weights.values():
        local.start()

    barrier = pltpu.get_barrier_semaphore()
    greeted = 0
    for up in sorted({0, 1, n_lat - 1}):
        for along in range(n_lon):
            for channel in (ch, near):
                if up == 0 and along == 0 and channel is ch:
                    continue
                pl.semaphore_signal(barrier, inc=1, device_id=device(up, along, channel), device_id_type=MESH)
                greeted += 1
    pl.semaphore_signal(barrier, inc=1, device_id=device(0, 0, far), device_id_type=MESH)
    pl.semaphore_wait(barrier, greeted + 1)
    for slot in (1, 0):
        weights[0, slot][1].start()

    def pack(act, conv):
        for j in range(n_lon):
            piece = act[:, j * part:(j + 1) * part]
            lower = jnp.concatenate(
                [piece[half:], jnp.zeros((2 * half - cells, part), jnp.float32)], axis=0
            )
            apack[conv, j] = jnp.concatenate([piece[:half], lower], axis=1).astype(jnp.bfloat16)
            fill = jnp.zeros((hpack.shape[3] - cols, part), jnp.float32)
            hpack[conv, 0, j] = jnp.concatenate([piece[cells - cols:], fill], axis=0).astype(jnp.bfloat16)
            hpack[conv, 1, j] = jnp.concatenate([piece[:cols], fill], axis=0).astype(jnp.bfloat16)

    def unpack(block):
        block = block.astype(jnp.float32)
        whole = jnp.concatenate([block[:, :part], block[:cells - half, part:]], axis=0)
        return whole.reshape(rows, cols, part)

    def main_copy(conv, p, k):
        return remote(
            apack.at[conv, (lon + k) % n_lon], arecv.at[conv, p, k],
            as_sem.at[conv, p, k], ar_sem.at[conv, p, k], device(0, k, (ch, near)[p]),
        )

    def halo_copy(conv, side, p, k):
        return remote(
            hpack.at[conv, side, (lon + k) % n_lon], hrecv.at[conv, side, p, k],
            hs_sem.at[conv, side, p, k], hr_sem.at[conv, side, p, k],
            device((1, -1)[side] % n_lat, k, (ch, near)[p]),
        )

    mains = [(p, k) for k in order for p in (0, 1) if (p, k) != (0, 0)]
    halos = [(p, k) for k in order for p in (0, 1)]
    sends = (lat < n_lat - 1, lat > 0)
    gets = (lat > 0, lat < n_lat - 1)

    def exchange(conv):
        for p, k in mains:
            main_copy(conv, p, k).start()
        for side in (0, 1):
            @pl.when(sends[side])
            def _():
                for p, k in halos:
                    halo_copy(conv, side, p, k).start()

    def assemble(conv):
        def place(k):
            return pl.ds(pl.multiple_of(EDGE + ((lon - k + n_lon) % n_lon) * cols, 8), cols)

        def lanes(p):
            return slice(p * part, (p + 1) * part)

        field[1:rows + 1, place(0), lanes(0)] = unpack(apack[conv, lon])
        for p, k in mains:
            main_copy(conv, p, k).wait_recv()
            field[1:rows + 1, place(k), lanes(p)] = unpack(arecv[conv, p, k])
        for side in (0, 1):
            row, inner = ((0, 1), (rows + 1, rows))[side]

            @pl.when(gets[side])
            def _():
                for p, k in halos:
                    halo_copy(conv, side, p, k).wait_recv()
                    field[row, place(k), lanes(p)] = hrecv[conv, side, p, k].astype(jnp.float32)[:cols]

            @pl.when(jnp.logical_not(gets[side]))
            def _():
                turn = all_cols // 2
                field[row, EDGE:EDGE + turn] = field[inner, EDGE + turn:EDGE + all_cols]
                field[row, EDGE + turn:EDGE + all_cols] = field[inner, EDGE:EDGE + turn]

        field[:, EDGE - 1:EDGE] = field[:, EDGE + all_cols - 1:EDGE + all_cols]
        field[:, EDGE + all_cols:EDGE + all_cols + 1] = field[:, EDGE:EDGE + 1]
        for e in range(3):
            taps[:, :, e * 2 * part:(e + 1) * 2 * part] = field[
                :, EDGE - 1 + e:EDGE - 1 + e + all_cols
            ].astype(jnp.bfloat16)

    def multiply(conv, slot):
        local, other = weights[conv, slot]
        local.wait()
        other.wait_recv()
        total = None
        for a in range(3):
            term = jnp.dot(
                taps[a:a + rows].reshape(rows * all_cols, 6 * part),
                w[conv, slot, a].reshape(6 * part, width),
                preferred_element_type=jnp.float32,
            )
            total = term if total is None else total + term
        acc[slot] = total.reshape(rows, all_cols, width)

    def chunk(slot, k):
        start = pl.multiple_of(((lon + k) % n_lon) * cols, 8)
        return acc[slot, :, pl.ds(start, cols), :].reshape(cells, width)

    def padded(value):
        fill = jnp.zeros((ysend.shape[2] - cells, width), jnp.float32)
        return jnp.concatenate([value, fill], axis=0).astype(jnp.bfloat16)

    def far_copy(conv, k):
        return remote(
            ysend.at[conv, k], yrecv.at[conv, k], ys_sem.at[conv, k], yr_sem.at[conv, k],
            device(0, 0, far),
        )

    def along_copy(conv, k):
        return remote(
            zsend.at[conv, k], zrecv.at[conv, k], zs_sem.at[conv, k], zr_sem.at[conv, k],
            device(0, k, ch),
        )

    def conv_sum(conv, bias):
        assemble(conv)
        multiply(conv, 1)
        for k in order:
            ysend[conv, k] = padded(chunk(1, k))
            far_copy(conv, k).start()
        multiply(conv, 0)
        total = None
        for k in order:
            far_copy(conv, k).wait_recv()
            value = chunk(0, k) + yrecv[conv, k].astype(jnp.float32)[:cells]
            if k:
                zsend[conv, k] = padded(value)
                along_copy(conv, k).start()
            else:
                total = value
        for k in order[:-1]:
            along_copy(conv, k).wait_recv()
            total = total + zrecv[conv, k].astype(jnp.float32)[:cells]
        return total + bias

    features = x_ref[0].astype(jnp.float32).reshape(cells, width)
    pack(silu(features), 0)
    exchange(0)
    for slot in (1, 0):
        weights[1, slot][1].start()
    hidden = conv_sum(0, b1_ref[...])
    pack(silu(hidden), 1)
    exchange(1)
    second = conv_sum(1, b2_ref[...])
    features = x_ref[0].astype(jnp.float32).reshape(cells, width)
    result = (features + second) * skip_scale
    out_ref[0] = result.reshape(rows, cols, width).astype(jnp.bfloat16)

    for conv in (0, 1):
        for slot in (0, 1):
            weights[conv, slot][1].wait_send()
        for p, k in mains:
            main_copy(conv, p, k).wait_send()
        for side in (0, 1):
            @pl.when(sends[side])
            def _():
                for p, k in halos:
                    halo_copy(conv, side, p, k).wait_send()
        for k in order:
            far_copy(conv, k).wait_send()
            if k:
                along_copy(conv, k).wait_send()


def body(n_lat, n_lon, features, kernel_one, bias_one, kernel_two, bias_two):
    _, rows, cols, width = features.shape
    cells, part, all_cols = rows * cols, width // n_lon, cols * n_lon
    half = round_up(-(-cells // 2), 16)
    tall = round_up(cells, 16)
    bf16, f32 = jnp.bfloat16, jnp.float32
    dma = pltpu.SemaphoreType.DMA
    vmem = pl.BlockSpec(memory_space=pltpu.VMEM)
    anywhere = pl.BlockSpec(memory_space=pl.ANY)
    return pl.pallas_call(
        functools.partial(block_kernel, n_lat, n_lon),
        out_shape=jax.ShapeDtypeStruct(features.shape, bf16),
        in_specs=[vmem, anywhere, vmem, anywhere, vmem],
        out_specs=vmem,
        scratch_shapes=[
            pltpu.VMEM((2, 2, 3, 3, 2, part, width), bf16),
            pltpu.VMEM((2, n_lon, half, 2 * part), bf16),
            pltpu.VMEM((2, 2, n_lon, half, 2 * part), bf16),
            pltpu.VMEM((2, 2, n_lon, round_up(cols, 16), part), bf16),
            pltpu.VMEM((2, 2, 2, n_lon, round_up(cols, 16), part), bf16),
            pltpu.VMEM((rows + 2, all_cols + 2 * EDGE, 2 * part), f32),
            pltpu.VMEM((rows + 2, all_cols, 6 * part), bf16),
            pltpu.VMEM((2, rows, all_cols, width), f32),
            pltpu.VMEM((2, n_lon, tall, width), bf16),
            pltpu.VMEM((2, n_lon, tall, width), bf16),
            pltpu.VMEM((2, n_lon, tall, width), bf16),
            pltpu.VMEM((2, n_lon, tall, width), bf16),
            dma((2, 2)), dma((2, 2)), dma((2, 2)),
            dma((2, 2, n_lon)), dma((2, 2, n_lon)),
            dma((2, 2, 2, n_lon)), dma((2, 2, 2, n_lon)),
            dma((2, n_lon)), dma((2, n_lon)), dma((2, n_lon)), dma((2, n_lon)),
        ],
        compiler_params=pltpu.CompilerParams(
            collective_id=0, has_side_effects=True, vmem_limit_bytes=56 * 2**20
        ),
        name="residual_block",
    )(features, kernel_one, bias_one.reshape(1, width), kernel_two, bias_two.reshape(1, width))


def solution(mesh):
    placed = (
        P(None, "lat", "lon", "ch"),
        P(None, None, "ch", "lon", None),
        P("ch"),
        P(None, None, "ch", "lon", None),
        P("ch"),
    )
    return jax.shard_map(
        functools.partial(body, mesh.shape["lat"], mesh.shape["lon"]),
        mesh=mesh, in_specs=placed, out_specs=P(None, "lat", "lon", "ch"), check_vma=False,
    )
```

```python
import functools

import jax
import jax.numpy as jnp
from jax import lax
from jax.experimental import pallas as pl
from jax.experimental.pallas import tpu as pltpu
from jax.sharding import PartitionSpec as P

skip_scale = 0.7071067811865476
MESH = pl.DeviceIdType.MESH
EDGE = 8


def round_up(value, step):
    return -(-value // step) * step


def silu(value):
    return value / (1.0 + jnp.exp(-value))


def block_kernel(
    n_lat, n_lon, x_ref, k1_ref, b1_ref, k2_ref, b2_ref, out_ref,
    w, apack, arecv, hpack, hrecv, field, taps, acc, ysend, yrecv, zsend, zrecv,
    wl_sem, ws_sem, wr_sem, as_sem, ar_sem, hs_sem, hr_sem, fs_sem, fr_sem, ys_sem, yr_sem, zs_sem, zr_sem,
):
    rows, cols, width = x_ref.shape[1:]
    cells = rows * cols
    part = width // n_lon
    half = apack.shape[2]
    all_cols = cols * n_lon
    lat, lon, ch = lax.axis_index("lat"), lax.axis_index("lon"), lax.axis_index("ch")
    near = ch + 1 - 2 * (ch % 2)
    far = ch + 2 - 4 * ((ch // 2) % 2)
    near_far = near + 2 - 4 * ((near // 2) % 2)
    order = list(range(1, n_lon)) + [0]

    def device(up, along, channel):
        return {"lat": (lat + up) % n_lat, "lon": (lon + along) % n_lon, "ch": channel}

    def remote(src, dst, send, recv, target):
        return pltpu.make_async_remote_copy(
            src_ref=src, dst_ref=dst, send_sem=send, recv_sem=recv,
            device_id=target, device_id_type=MESH,
        )

    def weight_copies(conv, slot):
        source = (k1_ref, k2_ref)[conv]
        mine, theirs = ((ch, near), (far, near_far))[slot]

        def outputs(group):
            return source.at[:, :, 0, :, pl.ds(pl.multiple_of(group * width, width), width)]

        return (
            pltpu.make_async_copy(outputs(mine), w.at[conv, slot, :, :, 0], wl_sem.at[conv, slot]),
            remote(
                outputs(theirs), w.at[conv, slot, :, :, 1],
                ws_sem.at[conv, slot], wr_sem.at[conv, slot], device(0, 0, near),
            ),
        )

    weights = {(conv, slot): weight_copies(conv, slot) for conv in (0, 1) for slot in (1, 0)}
    for local, _ in weights.values():
        local.start()

    barrier = pltpu.get_barrier_semaphore()
    greeted = 0
    peers = [(up, along, ch) for up in sorted({0, 1, n_lat - 1}) for along in range(n_lon) if up or along]
    for peer in peers + [(0, 0, near), (0, 0, far)]:
        pl.semaphore_signal(barrier, inc=1, device_id=device(*peer), device_id_type=MESH)
        greeted += 1

    def pack(act, conv):
        for j in range(n_lon):
            piece = act[:, j * part:(j + 1) * part]
            lower = jnp.concatenate(
                [piece[half:], jnp.zeros((2 * half - cells, part), jnp.float32)], axis=0
            )
            apack[conv, j] = jnp.concatenate([piece[:half], lower], axis=1).astype(jnp.bfloat16)
            fill = jnp.zeros((hpack.shape[3] - cols, part), jnp.float32)
            hpack[conv, 0, j] = jnp.concatenate([piece[cells - cols:], fill], axis=0).astype(jnp.bfloat16)
            hpack[conv, 1, j] = jnp.concatenate([piece[:cols], fill], axis=0).astype(jnp.bfloat16)

    def unpack(block):
        block = block.astype(jnp.float32)
        whole = jnp.concatenate([block[:, :part], block[:cells - half, part:]], axis=0)
        return whole.reshape(rows, cols, part)

    def main_copy(conv, k):
        return remote(
            apack.at[conv, (lon + k) % n_lon], arecv.at[conv, 0, k],
            as_sem.at[conv, 0, k], ar_sem.at[conv, 0, k], device(0, k, ch),
        )

    def forward_copy(conv, k):
        return remote(
            arecv.at[conv, 0, k] if k else apack.at[conv, lon], arecv.at[conv, 1, k],
            as_sem.at[conv, 1, k], ar_sem.at[conv, 1, k], device(0, 0, near),
        )

    def halo_copy(conv, side, k):
        return remote(
            hpack.at[conv, side, (lon + k) % n_lon], hrecv.at[conv, side, 0, k],
            hs_sem.at[conv, side, k], hr_sem.at[conv, side, k],
            device((1, -1)[side] % n_lat, k, ch),
        )

    def halo_forward(conv, side):
        return remote(
            hrecv.at[conv, side, 0], hrecv.at[conv, side, 1],
            fs_sem.at[conv, side], fr_sem.at[conv, side], device(0, 0, near),
        )

    sends = (lat < n_lat - 1, lat > 0)
    gets = (lat > 0, lat < n_lat - 1)

    def exchange(conv):
        for k in order[:-1]:
            main_copy(conv, k).start()
        for side in (0, 1):
            @pl.when(sends[side])
            def _():
                for k in order:
                    halo_copy(conv, side, k).start()
        forward_copy(conv, 0).start()

    def assemble(conv):
        def place(k):
            return pl.ds(pl.multiple_of(EDGE + ((lon - k + n_lon) % n_lon) * cols, 8), cols)

        def lanes(p):
            return slice(p * part, (p + 1) * part)

        field[1:rows + 1, place(0), lanes(0)] = unpack(apack[conv, lon])
        for k in order[:-1]:
            main_copy(conv, k).wait_recv()
            forward_copy(conv, k).start()
            field[1:rows + 1, place(k), lanes(0)] = unpack(arecv[conv, 0, k])
        for side in (0, 1):
            @pl.when(gets[side])
            def _():
                for k in order:
                    halo_copy(conv, side, k).wait_recv()
                halo_forward(conv, side).start()
        for k in [0] + order[:-1]:
            forward_copy(conv, k).wait_recv()
            field[1:rows + 1, place(k), lanes(1)] = unpack(arecv[conv, 1, k])
        for side in (0, 1):
            row, inner = ((0, 1), (rows + 1, rows))[side]

            @pl.when(gets[side])
            def _():
                halo_forward(conv, side).wait_recv()
                for p in (0, 1):
                    for k in order:
                        field[row, place(k), lanes(p)] = hrecv[conv, side, p, k].astype(jnp.float32)[:cols]

            @pl.when(jnp.logical_not(gets[side]))
            def _():
                turn = all_cols // 2
                field[row, EDGE:EDGE + turn] = field[inner, EDGE + turn:EDGE + all_cols]
                field[row, EDGE + turn:EDGE + all_cols] = field[inner, EDGE:EDGE + turn]

        field[:, EDGE - 1:EDGE] = field[:, EDGE + all_cols - 1:EDGE + all_cols]
        field[:, EDGE + all_cols:EDGE + all_cols + 1] = field[:, EDGE:EDGE + 1]
        for e in range(3):
            taps[:, :, e * 2 * part:(e + 1) * 2 * part] = field[
                :, EDGE - 1 + e:EDGE - 1 + e + all_cols
            ].astype(jnp.bfloat16)

    def multiply(conv, slot):
        local, other = weights[conv, slot]
        local.wait()
        other.wait_recv()
        total = None
        for a in range(3):
            term = jnp.dot(
                taps[a:a + rows].reshape(rows * all_cols, 6 * part),
                w[conv, slot, a].reshape(6 * part, width),
                preferred_element_type=jnp.float32,
            )
            total = term if total is None else total + term
        acc[slot] = total.reshape(rows, all_cols, width)

    def chunk(slot, k):
        start = pl.multiple_of(((lon + k) % n_lon) * cols, 8)
        return acc[slot, :, pl.ds(start, cols), :].reshape(cells, width)

    def padded(value):
        fill = jnp.zeros((ysend.shape[2] - cells, width), jnp.float32)
        return jnp.concatenate([value, fill], axis=0).astype(jnp.bfloat16)

    def far_copy(conv, k):
        return remote(
            ysend.at[conv, k], yrecv.at[conv, k], ys_sem.at[conv, k], yr_sem.at[conv, k],
            device(0, 0, far),
        )

    def along_copy(conv, k):
        return remote(
            zsend.at[conv, k], zrecv.at[conv, k], zs_sem.at[conv, k], zr_sem.at[conv, k],
            device(0, k, ch),
        )

    def conv_sum(conv, bias):
        assemble(conv)
        multiply(conv, 1)
        for k in order:
            ysend[conv, k] = padded(chunk(1, k))
            far_copy(conv, k).start()
        multiply(conv, 0)
        if conv == 0:
            for slot in (1, 0):
                weights[1, slot][1].start()
        total = None
        for k in order:
            far_copy(conv, k).wait_recv()
            value = chunk(0, k) + yrecv[conv, k].astype(jnp.float32)[:cells]
            if k:
                zsend[conv, k] = padded(value)
                along_copy(conv, k).start()
            else:
                total = value
        for k in order[:-1]:
            along_copy(conv, k).wait_recv()
            total = total + zrecv[conv, k].astype(jnp.float32)[:cells]
        return total + bias

    features = x_ref[0].astype(jnp.float32).reshape(cells, width)
    pack(silu(features), 0)
    pl.semaphore_wait(barrier, greeted)
    for slot in (1, 0):
        weights[0, slot][1].start()
    exchange(0)
    hidden = conv_sum(0, b1_ref[...])
    pack(silu(hidden), 1)
    exchange(1)
    second = conv_sum(1, b2_ref[...])
    features = x_ref[0].astype(jnp.float32).reshape(cells, width)
    result = (features + second) * skip_scale
    out_ref[0] = result.reshape(rows, cols, width).astype(jnp.bfloat16)

    for conv in (0, 1):
        for slot in (0, 1):
            weights[conv, slot][1].wait_send()
        for k in order:
            forward_copy(conv, k).wait_send()
            if k:
                main_copy(conv, k).wait_send()
        for side in (0, 1):
            @pl.when(sends[side])
            def _():
                for k in order:
                    halo_copy(conv, side, k).wait_send()

            @pl.when(gets[side])
            def _():
                halo_forward(conv, side).wait_send()
        for k in order:
            far_copy(conv, k).wait_send()
            if k:
                along_copy(conv, k).wait_send()


def body(n_lat, n_lon, features, kernel_one, bias_one, kernel_two, bias_two):
    _, rows, cols, width = features.shape
    cells, part, all_cols = rows * cols, width // n_lon, cols * n_lon
    half = round_up(-(-cells // 2), 16)
    tall = round_up(cells, 16)
    bf16, f32 = jnp.bfloat16, jnp.float32
    dma = pltpu.SemaphoreType.DMA
    vmem = pl.BlockSpec(memory_space=pltpu.VMEM)
    anywhere = pl.BlockSpec(memory_space=pl.ANY)
    return pl.pallas_call(
        functools.partial(block_kernel, n_lat, n_lon),
        out_shape=jax.ShapeDtypeStruct(features.shape, bf16),
        in_specs=[vmem, anywhere, vmem, anywhere, vmem],
        out_specs=vmem,
        scratch_shapes=[
            pltpu.VMEM((2, 2, 3, 3, 2, part, width), bf16),
            pltpu.VMEM((2, n_lon, half, 2 * part), bf16),
            pltpu.VMEM((2, 2, n_lon, half, 2 * part), bf16),
            pltpu.VMEM((2, 2, n_lon, round_up(cols, 16), part), bf16),
            pltpu.VMEM((2, 2, 2, n_lon, round_up(cols, 16), part), bf16),
            pltpu.VMEM((rows + 2, all_cols + 2 * EDGE, 2 * part), f32),
            pltpu.VMEM((rows + 2, all_cols, 6 * part), bf16),
            pltpu.VMEM((2, rows, all_cols, width), f32),
            pltpu.VMEM((2, n_lon, tall, width), bf16),
            pltpu.VMEM((2, n_lon, tall, width), bf16),
            pltpu.VMEM((2, n_lon, tall, width), bf16),
            pltpu.VMEM((2, n_lon, tall, width), bf16),
            dma((2, 2)), dma((2, 2)), dma((2, 2)),
            dma((2, 2, n_lon)), dma((2, 2, n_lon)),
            dma((2, 2, n_lon)), dma((2, 2, n_lon)), dma((2, 2)), dma((2, 2)),
            dma((2, n_lon)), dma((2, n_lon)), dma((2, n_lon)), dma((2, n_lon)),
        ],
        compiler_params=pltpu.CompilerParams(
            collective_id=0, has_side_effects=True, vmem_limit_bytes=56 * 2**20
        ),
        name="residual_block",
    )(features, kernel_one, bias_one.reshape(1, width), kernel_two, bias_two.reshape(1, width))


def solution(mesh):
    placed = (
        P(None, "lat", "lon", "ch"),
        P(None, None, "ch", "lon", None),
        P("ch"),
        P(None, None, "ch", "lon", None),
        P("ch"),
    )
    return jax.shard_map(
        functools.partial(body, mesh.shape["lat"], mesh.shape["lon"]),
        mesh=mesh, in_specs=placed, out_specs=P(None, "lat", "lon", "ch"), check_vma=False,
    )
```

```python
import functools

import jax
import jax.numpy as jnp
from jax import lax
from jax.experimental import pallas as pl
from jax.experimental.pallas import tpu as pltpu
from jax.sharding import PartitionSpec as P

skip_scale = 0.7071067811865476
MESH = pl.DeviceIdType.MESH
EDGE = 8


def round_up(value, step):
    return -(-value // step) * step


def silu(value):
    return value / (1.0 + jnp.exp(-value))


def pack(value, half):
    count, part = value.shape
    lower = value[half:]
    if 2 * half > count:
        lower = jnp.concatenate([lower, jnp.zeros((2 * half - count, part), value.dtype)], axis=0)
    return jnp.concatenate([value[:half], lower], axis=1)


def unpack(block, count):
    half, part = block.shape[0], block.shape[1] // 2
    return jnp.concatenate([block[:, :part], block[:count - half, part:]], axis=0)


def block_kernel(
    n_lat, n_lon, x_ref, k1_ref, b1_ref, k2_ref, b2_ref, out_ref,
    w, apack, arecv, hpack, hrecv, bpack, brecv, epack, erecv, field, taps,
    own, ysend1, yrecv1, zsend1, zrecv1, acc, ysend2, yrecv2, zsend2, zrecv2,
    wl_sem, ws_sem, wr_sem, as_sem, ar_sem, hs_sem, hr_sem, fs_sem, fr_sem,
    bs_sem, br_sem, es_sem, er_sem, ys_sem, yr_sem, zs_sem, zr_sem,
):
    rows, cols, width = x_ref.shape[1:]
    cells = rows * cols
    part = width // n_lon
    half = apack.shape[1]
    all_cols = cols * n_lon
    all_cells = rows * all_cols
    band_half = bpack.shape[0]
    f32, bf16 = jnp.float32, jnp.bfloat16
    lat, lon, ch = lax.axis_index("lat"), lax.axis_index("lon"), lax.axis_index("ch")
    near = ch + 1 - 2 * (ch % 2)
    far = ch + 2 - 4 * ((ch // 2) % 2)
    near_far = near + 2 - 4 * ((near // 2) % 2)
    away = list(range(1, n_lon))
    order = away + [0]

    def device(up, along, channel):
        return {"lat": (lat + up) % n_lat, "lon": (lon + along) % n_lon, "ch": channel}

    def remote(src, dst, send, recv, target):
        return pltpu.make_async_remote_copy(
            src_ref=src, dst_ref=dst, send_sem=send, recv_sem=recv,
            device_id=target, device_id_type=MESH,
        )

    def weight_copies(conv, slot):
        source = (k1_ref, k2_ref)[conv]
        mine, theirs = ((ch, near), (far, near_far))[slot]

        def outputs(group):
            return source.at[:, :, 0, :, pl.ds(pl.multiple_of(group * width, width), width)]

        return (
            pltpu.make_async_copy(outputs(mine), w.at[conv, slot, :, :, 0], wl_sem.at[conv, slot]),
            remote(
                outputs(theirs), w.at[conv, slot, :, :, 1],
                ws_sem.at[conv, slot], wr_sem.at[conv, slot], device(0, 0, near),
            ),
        )

    weights = {(conv, slot): weight_copies(conv, slot) for conv in (0, 1) for slot in (1, 0)}
    for local, _ in weights.values():
        local.start()

    barrier = pltpu.get_barrier_semaphore()
    greeted = 0
    ups = sorted({0, 1, n_lat - 1})
    peers = [(up, along, ch) for up in ups for along in range(n_lon) if up or along]
    peers += [(up, 0, near) for up in ups] + [(0, 0, far)]
    for peer in peers:
        pl.semaphore_signal(barrier, inc=1, device_id=device(*peer), device_id_type=MESH)
        greeted += 1

    sends = (lat < n_lat - 1, lat > 0)
    gets = (lat > 0, lat < n_lat - 1)

    def main_copy(k):
        return remote(
            apack.at[(lon + k) % n_lon], arecv.at[0, k], as_sem.at[0, k], ar_sem.at[0, k], device(0, k, ch)
        )

    def forward_copy(k):
        return remote(
            arecv.at[0, k] if k else apack.at[lon], arecv.at[1, k],
            as_sem.at[1, k], ar_sem.at[1, k], device(0, 0, near),
        )

    def halo_copy(side, k):
        return remote(
            hpack.at[side, (lon + k) % n_lon], hrecv.at[side, 0, k],
            hs_sem.at[side, k], hr_sem.at[side, k], device((1, -1)[side] % n_lat, k, ch),
        )

    def halo_forward(side):
        return remote(
            hrecv.at[side, 0], hrecv.at[side, 1], fs_sem.at[side], fr_sem.at[side], device(0, 0, near)
        )

    def band_copy():
        return remote(bpack, brecv, bs_sem, br_sem, device(0, 0, near))

    def edge_copy(side, p):
        return remote(
            epack.at[side], erecv.at[side, p], es_sem.at[side, p], er_sem.at[side, p],
            device((1, -1)[side] % n_lat, 0, (ch, near)[p]),
        )

    def far_copy(conv, k):
        src, dst = ((ysend1, yrecv1), (ysend2, yrecv2))[conv]
        slot = (lon + k) % n_lon
        return remote(src.at[slot], dst.at[slot], ys_sem.at[conv, k], yr_sem.at[conv, k], device(0, 0, far))

    def along_copy(conv, k):
        src, dst = ((zsend1, zrecv1), (zsend2, zrecv2))[conv]
        return remote(src.at[k], dst.at[k], zs_sem.at[conv, k], zr_sem.at[conv, k], device(0, k, ch))

    def lanes(p):
        return slice(p * part, (p + 1) * part)

    inside = slice(EDGE, EDGE + all_cols)

    def fold(side):
        row, inner = ((0, 1), (rows + 1, rows))[side]
        turn = all_cols // 2
        field[row, EDGE:EDGE + turn] = field[inner, EDGE + turn:EDGE + all_cols]
        field[row, EDGE + turn:EDGE + all_cols] = field[inner, EDGE:EDGE + turn]

    def spread():
        field[:, EDGE - 1:EDGE] = field[:, EDGE + all_cols - 1:EDGE + all_cols]
        field[:, EDGE + all_cols:EDGE + all_cols + 1] = field[:, EDGE:EDGE + 1]
        for e in range(3):
            taps[:, :, e * 2 * part:(e + 1) * 2 * part] = field[
                :, EDGE - 1 + e:EDGE - 1 + e + all_cols
            ].astype(bf16)

    def exchange_one():
        for k in away:
            main_copy(k).start()
        for side in (0, 1):
            @pl.when(sends[side])
            def _():
                for k in order:
                    halo_copy(side, k).start()
        forward_copy(0).start()

    def assemble_one():
        def place(k):
            return pl.ds(pl.multiple_of(EDGE + ((lon - k + n_lon) % n_lon) * cols, 8), cols)

        def cell_block(block):
            return unpack(block.astype(f32), cells).reshape(rows, cols, part)

        field[1:rows + 1, place(0), lanes(0)] = cell_block(apack[lon])
        for k in away:
            main_copy(k).wait_recv()
            forward_copy(k).start()
            field[1:rows + 1, place(k), lanes(0)] = cell_block(arecv[0, k])
        for side in (0, 1):
            @pl.when(gets[side])
            def _():
                for k in order:
                    halo_copy(side, k).wait_recv()
                halo_forward(side).start()
        for k in [0] + away:
            forward_copy(k).wait_recv()
            field[1:rows + 1, place(k), lanes(1)] = cell_block(arecv[1, k])
        for side in (0, 1):
            @pl.when(gets[side])
            def _():
                halo_forward(side).wait_recv()
                for p in (0, 1):
                    for k in order:
                        field[(0, rows + 1)[side], place(k), lanes(p)] = hrecv[side, p, k].astype(f32)[:cols]

            @pl.when(jnp.logical_not(gets[side]))
            def _():
                fold(side)
        spread()

    def assemble_two(act):
        bpack[...] = act.astype(bf16)
        band_copy().start()
        band = unpack(act, all_cells)
        epack[0] = band[all_cells - all_cols:].astype(bf16)
        epack[1] = band[:all_cols].astype(bf16)
        for side in (0, 1):
            @pl.when(sends[side])
            def _():
                for p in (1, 0):
                    edge_copy(side, p).start()
        field[1:rows + 1, inside, lanes(0)] = band.reshape(rows, all_cols, part)
        band_copy().wait_recv()
        other = unpack(brecv[...].astype(f32), all_cells)
        field[1:rows + 1, inside, lanes(1)] = other.reshape(rows, all_cols, part)
        for side in (0, 1):
            @pl.when(gets[side])
            def _():
                for p in (0, 1):
                    edge_copy(side, p).wait_recv()
                    field[(0, rows + 1)[side], inside, lanes(p)] = erecv[side, p].astype(f32)

            @pl.when(jnp.logical_not(gets[side]))
            def _():
                fold(side)
        spread()

    def multiply(conv, slot):
        local, other = weights[conv, slot]
        local.wait()
        other.wait_recv()
        total = None
        for a in range(3):
            term = jnp.dot(
                taps[a:a + rows].reshape(all_cells, 6 * part),
                w[conv, slot, a].reshape(6 * part, width),
                preferred_element_type=f32,
            )
            total = term if total is None else total + term
        return total

    features = x_ref[0].astype(f32).reshape(cells, width)
    act = silu(features)
    fill = jnp.zeros((hpack.shape[2] - cols, part), f32)
    for j in range(n_lon):
        piece = act[:, lanes(j)]
        apack[j] = pack(piece, half).astype(bf16)
        hpack[0, j] = jnp.concatenate([piece[cells - cols:], fill], axis=0).astype(bf16)
        hpack[1, j] = jnp.concatenate([piece[:cols], fill], axis=0).astype(bf16)
    pl.semaphore_wait(barrier, greeted)
    for slot in (1, 0):
        weights[0, slot][1].start()
    exchange_one()
    assemble_one()

    total = multiply(0, 1)
    for j in range(n_lon):
        ysend1[j] = pack(total[:, lanes(j)], band_half).astype(bf16)
    for k in order:
        far_copy(0, k).start()
    total = multiply(0, 0)
    for j in range(n_lon):
        own[j] = pack(total[:, lanes(j)], band_half)
    for slot in (1, 0):
        weights[1, slot][1].start()
    hidden = None
    for k in order:
        far_copy(0, k).wait_recv()
        slot = (lon + k) % n_lon
        value = own[slot] + yrecv1[slot].astype(f32)
        if k:
            zsend1[k] = value.astype(bf16)
            along_copy(0, k).start()
        else:
            hidden = value
    for k in away:
        along_copy(0, k).wait_recv()
        hidden = hidden + zrecv1[k].astype(f32)
    bias = b1_ref[:, lanes(0)]
    for j in away:
        bias = jnp.where(lon == j, b1_ref[:, lanes(j)], bias)
    assemble_two(silu(hidden + jnp.concatenate([bias, bias], axis=1)))

    def chunk(slot, k):
        start = pl.multiple_of(((lon + k) % n_lon) * cols, 8)
        return acc[slot, :, pl.ds(start, cols), :].reshape(cells, width)

    def padded(value):
        spare = jnp.zeros((ysend2.shape[1] - cells, width), f32)
        return jnp.concatenate([value, spare], axis=0).astype(bf16)

    acc[1] = multiply(1, 1).reshape(rows, all_cols, width)
    for k in order:
        ysend2[(lon + k) % n_lon] = padded(chunk(1, k))
        far_copy(1, k).start()
    acc[0] = multiply(1, 0).reshape(rows, all_cols, width)
    second = None
    for k in order:
        far_copy(1, k).wait_recv()
        value = chunk(0, k) + yrecv2[(lon + k) % n_lon].astype(f32)[:cells]
        if k:
            zsend2[k] = padded(value)
            along_copy(1, k).start()
        else:
            second = value
    for k in away:
        along_copy(1, k).wait_recv()
        second = second + zrecv2[k].astype(f32)[:cells]
    out_ref[0] = (second + b2_ref[...]).reshape(rows, cols, width)

    for k in order:
        forward_copy(k).wait_send()
        if k:
            main_copy(k).wait_send()
    band_copy().wait_send()
    for side in (0, 1):
        @pl.when(sends[side])
        def _():
            for k in order:
                halo_copy(side, k).wait_send()
            for p in (0, 1):
                edge_copy(side, p).wait_send()

        @pl.when(gets[side])
        def _():
            halo_forward(side).wait_send()
    for conv in (0, 1):
        for slot in (0, 1):
            weights[conv, slot][1].wait_send()
        for k in order:
            far_copy(conv, k).wait_send()
            if k:
                along_copy(conv, k).wait_send()


def body(n_lat, n_lon, features, kernel_one, bias_one, kernel_two, bias_two):
    _, rows, cols, width = features.shape
    cells, part, all_cols = rows * cols, width // n_lon, cols * n_lon
    half = round_up(-(-cells // 2), 16)
    band_half = round_up(-(-rows * all_cols // 2), 16)
    tall, short = round_up(cells, 16), round_up(cols, 16)
    bf16, f32 = jnp.bfloat16, jnp.float32
    dma = pltpu.SemaphoreType.DMA
    vmem = pl.BlockSpec(memory_space=pltpu.VMEM)
    anywhere = pl.BlockSpec(memory_space=pl.ANY)
    second = pl.pallas_call(
        functools.partial(block_kernel, n_lat, n_lon),
        out_shape=jax.ShapeDtypeStruct(features.shape, f32),
        in_specs=[vmem, anywhere, vmem, anywhere, vmem],
        out_specs=vmem,
        scratch_shapes=[
            pltpu.VMEM((2, 2, 3, 3, 2, part, width), bf16),
            pltpu.VMEM((n_lon, half, 2 * part), bf16),
            pltpu.VMEM((2, n_lon, half, 2 * part), bf16),
            pltpu.VMEM((2, n_lon, short, part), bf16),
            pltpu.VMEM((2, 2, n_lon, short, part), bf16),
            pltpu.VMEM((band_half, 2 * part), bf16),
            pltpu.VMEM((band_half, 2 * part), bf16),
            pltpu.VMEM((2, all_cols, part), bf16),
            pltpu.VMEM((2, 2, all_cols, part), bf16),
            pltpu.VMEM((rows + 2, all_cols + 2 * EDGE, 2 * part), f32),
            pltpu.VMEM((rows + 2, all_cols, 6 * part), bf16),
            pltpu.VMEM((n_lon, band_half, 2 * part), f32),
            pltpu.VMEM((n_lon, band_half, 2 * part), bf16),
            pltpu.VMEM((n_lon, band_half, 2 * part), bf16),
            pltpu.VMEM((n_lon, band_half, 2 * part), bf16),
            pltpu.VMEM((n_lon, band_half, 2 * part), bf16),
            pltpu.VMEM((2, rows, all_cols, width), f32),
            pltpu.VMEM((n_lon, tall, width), bf16),
            pltpu.VMEM((n_lon, tall, width), bf16),
            pltpu.VMEM((n_lon, tall, width), bf16),
            pltpu.VMEM((n_lon, tall, width), bf16),
            dma((2, 2)), dma((2, 2)), dma((2, 2)),
            dma((2, n_lon)), dma((2, n_lon)),
            dma((2, n_lon)), dma((2, n_lon)), dma((2,)), dma((2,)),
            dma, dma, dma((2, 2)), dma((2, 2)),
            dma((2, n_lon)), dma((2, n_lon)), dma((2, n_lon)), dma((2, n_lon)),
        ],
        compiler_params=pltpu.CompilerParams(
            collective_id=0, has_side_effects=True, vmem_limit_bytes=56 * 2**20
        ),
        name="residual_block",
    )(features, kernel_one, bias_one.reshape(1, width), kernel_two, bias_two.reshape(1, width))
    return ((features.astype(f32) + second) * skip_scale).astype(bf16)


def solution(mesh):
    placed = (
        P(None, "lat", "lon", "ch"),
        P(None, None, "ch", "lon", None),
        P("ch"),
        P(None, None, "ch", "lon", None),
        P("ch"),
    )
    return jax.shard_map(
        functools.partial(body, mesh.shape["lat"], mesh.shape["lon"]),
        mesh=mesh, in_specs=placed, out_specs=P(None, "lat", "lon", "ch"), check_vma=False,
    )
```

```python
import functools

import jax
import jax.numpy as jnp
from jax import lax
from jax.experimental import pallas as pl
from jax.experimental.pallas import tpu as pltpu
from jax.sharding import PartitionSpec as P

skip_scale = 0.7071067811865476
MESH = pl.DeviceIdType.MESH
EDGE = 8


def round_up(value, step):
    return -(-value // step) * step


def silu(value):
    return value / (1.0 + jnp.exp(-value))


def pack(value, half):
    count, part = value.shape
    lower = value[half:]
    if 2 * half > count:
        lower = jnp.concatenate([lower, jnp.zeros((2 * half - count, part), value.dtype)], axis=0)
    return jnp.concatenate([value[:half], lower], axis=1)


def unpack(block, count):
    half, part = block.shape[0], block.shape[1] // 2
    return jnp.concatenate([block[:, :part], block[:count - half, part:]], axis=0)


def row_groups(rows, per_row, packed):
    groups, offset, first = [], 0, 0
    for count in (-(-rows // 2), rows // 2):
        size = round_up(-(-count * per_row // packed), 16)
        groups.append((first, count, offset, size))
        first, offset = first + count, offset + size
    return groups, offset


def block_kernel(
    n_lat, n_lon, x_ref, k1_ref, b1_ref, k2_ref, b2_ref, out_ref,
    w, apack, arecv, hpack, hrecv, bpack, brecv, epack, erecv, field, taps,
    own, kept, ysend1, yrecv1, zsend1, zrecv1, acc, ysend2, yrecv2, zsend2, zrecv2,
    wl_sem, ws_sem, wr_sem, as_sem, ar_sem, hs_sem, hr_sem, fs_sem, fr_sem,
    bs_sem, br_sem, es_sem, er_sem, ys_sem, yr_sem, zs_sem, zr_sem,
):
    rows, cols, width = x_ref.shape[1:]
    cells = rows * cols
    part = width // n_lon
    half = apack.shape[1]
    all_cols = cols * n_lon
    bands = row_groups(rows, all_cols, 2)[0]
    blocks = row_groups(rows, cols, 1)[0]
    f32, bf16 = jnp.float32, jnp.bfloat16
    lat, lon, ch = lax.axis_index("lat"), lax.axis_index("lon"), lax.axis_index("ch")
    near = ch + 1 - 2 * (ch % 2)
    far = ch + 2 - 4 * ((ch // 2) % 2)
    near_far = near + 2 - 4 * ((near // 2) % 2)
    away = list(range(1, n_lon))
    order = away + [0]

    def device(up, along, channel):
        return {"lat": (lat + up) % n_lat, "lon": (lon + along) % n_lon, "ch": channel}

    def remote(src, dst, send, recv, target):
        return pltpu.make_async_remote_copy(
            src_ref=src, dst_ref=dst, send_sem=send, recv_sem=recv,
            device_id=target, device_id_type=MESH,
        )

    def weight_copies(conv, slot):
        source = (k1_ref, k2_ref)[conv]
        mine, theirs = ((ch, near), (far, near_far))[slot]

        def outputs(group):
            return source.at[:, :, 0, :, pl.ds(pl.multiple_of(group * width, width), width)]

        return (
            pltpu.make_async_copy(outputs(mine), w.at[conv, slot, :, :, 0], wl_sem.at[conv, slot]),
            remote(
                outputs(theirs), w.at[conv, slot, :, :, 1],
                ws_sem.at[conv, slot], wr_sem.at[conv, slot], device(0, 0, near),
            ),
        )

    weights = {(conv, slot): weight_copies(conv, slot) for conv in (0, 1) for slot in (1, 0)}
    for local, _ in weights.values():
        local.start()

    barrier = pltpu.get_barrier_semaphore()
    greeted = 0
    ups = sorted({0, 1, n_lat - 1})
    peers = [(up, along, ch) for up in ups for along in range(n_lon) if up or along]
    peers += [(up, 0, near) for up in ups] + [(0, 0, far)]
    for peer in peers:
        pl.semaphore_signal(barrier, inc=1, device_id=device(*peer), device_id_type=MESH)
        greeted += 1

    sends = (lat < n_lat - 1, lat > 0)
    gets = (lat > 0, lat < n_lat - 1)

    def main_copy(k):
        return remote(
            apack.at[(lon + k) % n_lon], arecv.at[0, k], as_sem.at[0, k], ar_sem.at[0, k], device(0, k, ch)
        )

    def forward_copy(k):
        return remote(
            arecv.at[0, k] if k else apack.at[lon], arecv.at[1, k],
            as_sem.at[1, k], ar_sem.at[1, k], device(0, 0, near),
        )

    def halo_copy(side, k):
        return remote(
            hpack.at[side, (lon + k) % n_lon], hrecv.at[side, 0, k],
            hs_sem.at[side, k], hr_sem.at[side, k], device((1, -1)[side] % n_lat, k, ch),
        )

    def halo_forward(side):
        return remote(
            hrecv.at[side, 0], hrecv.at[side, 1], fs_sem.at[side], fr_sem.at[side], device(0, 0, near)
        )

    def band_copy(g):
        place = pl.ds(bands[g][2], bands[g][3])
        return remote(bpack.at[place], brecv.at[place], bs_sem.at[g], br_sem.at[g], device(0, 0, near))

    def edge_copy(side, p):
        return remote(
            epack.at[side], erecv.at[side, p], es_sem.at[side, p], er_sem.at[side, p],
            device((1, -1)[side] % n_lat, 0, (ch, near)[p]),
        )

    def piece_of(conv, g):
        return pl.ds(*(bands, blocks)[conv][g][2:])

    def far_copy(conv, g, k):
        src, dst = ((ysend1, yrecv1), (ysend2, yrecv2))[conv]
        slot, piece = (lon + k) % n_lon, piece_of(conv, g)
        return remote(
            src.at[slot, piece], dst.at[slot, piece],
            ys_sem.at[conv, g, k], yr_sem.at[conv, g, k], device(0, 0, far),
        )

    def along_copy(conv, g, k):
        src, dst = ((zsend1, zrecv1), (zsend2, zrecv2))[conv]
        piece = piece_of(conv, g)
        return remote(
            src.at[k, piece], dst.at[k, piece],
            zs_sem.at[conv, g, k], zr_sem.at[conv, g, k], device(0, k, ch),
        )

    def lanes(p):
        return slice(p * part, (p + 1) * part)

    inside = slice(EDGE, EDGE + all_cols)

    def fold(side):
        row, inner = ((0, 1), (rows + 1, rows))[side]
        turn = all_cols // 2
        field[row, EDGE:EDGE + turn] = field[inner, EDGE + turn:EDGE + all_cols]
        field[row, EDGE + turn:EDGE + all_cols] = field[inner, EDGE:EDGE + turn]

    def spread():
        field[:, EDGE - 1:EDGE] = field[:, EDGE + all_cols - 1:EDGE + all_cols]
        field[:, EDGE + all_cols:EDGE + all_cols + 1] = field[:, EDGE:EDGE + 1]
        for e in range(3):
            taps[:, :, e * 2 * part:(e + 1) * 2 * part] = field[
                :, EDGE - 1 + e:EDGE - 1 + e + all_cols
            ].astype(bf16)

    def exchange_one():
        for k in away:
            main_copy(k).start()
        for side in (0, 1):
            @pl.when(sends[side])
            def _():
                for k in order:
                    halo_copy(side, k).start()
        forward_copy(0).start()

    def assemble_one():
        def place(k):
            return pl.ds(pl.multiple_of(EDGE + ((lon - k + n_lon) % n_lon) * cols, 8), cols)

        def cell_block(block):
            return unpack(block.astype(f32), cells).reshape(rows, cols, part)

        field[1:rows + 1, place(0), lanes(0)] = cell_block(apack[lon])
        for k in away:
            main_copy(k).wait_recv()
            forward_copy(k).start()
            field[1:rows + 1, place(k), lanes(0)] = cell_block(arecv[0, k])
        for side in (0, 1):
            @pl.when(gets[side])
            def _():
                for k in order:
                    halo_copy(side, k).wait_recv()
                halo_forward(side).start()
        for k in [0] + away:
            forward_copy(k).wait_recv()
            field[1:rows + 1, place(k), lanes(1)] = cell_block(arecv[1, k])
        for side in (0, 1):
            @pl.when(gets[side])
            def _():
                halo_forward(side).wait_recv()
                for p in (0, 1):
                    for k in order:
                        field[(0, rows + 1)[side], place(k), lanes(p)] = hrecv[side, p, k].astype(f32)[:cols]

            @pl.when(jnp.logical_not(gets[side]))
            def _():
                fold(side)
        spread()

    def hand_on(g, act):
        first, count, offset, size = bands[g]
        bpack[offset:offset + size] = act.astype(bf16)
        band_copy(g).start()
        band = unpack(act, count * all_cols)
        for side in (0, 1):
            if g == (1, 0)[side]:
                epack[side] = (band[-all_cols:], band[:all_cols])[side].astype(bf16)

                @pl.when(sends[side])
                def _():
                    for p in (1, 0):
                        edge_copy(side, p).start()
        field[first + 1:first + 1 + count, inside, lanes(0)] = band.reshape(count, all_cols, part)

    def assemble_two():
        for g, (first, count, offset, size) in enumerate(bands):
            band_copy(g).wait_recv()
            other = unpack(brecv[offset:offset + size].astype(f32), count * all_cols)
            field[first + 1:first + 1 + count, inside, lanes(1)] = other.reshape(count, all_cols, part)
        for side in (0, 1):
            @pl.when(gets[side])
            def _():
                for p in (0, 1):
                    edge_copy(side, p).wait_recv()
                    field[(0, rows + 1)[side], inside, lanes(p)] = erecv[side, p].astype(f32)

            @pl.when(jnp.logical_not(gets[side]))
            def _():
                fold(side)
        spread()

    def weights_here(conv, slot):
        local, other = weights[conv, slot]
        local.wait()
        other.wait_recv()

    def multiply(conv, slot, g):
        first, count = bands[g][:2]
        total = None
        for a in range(3):
            term = jnp.dot(
                taps[first + a:first + a + count].reshape(count * all_cols, 6 * part),
                w[conv, slot, a].reshape(6 * part, width),
                preferred_element_type=f32,
            )
            total = term if total is None else total + term
        return total

    features = x_ref[0].astype(f32).reshape(cells, width)
    act = silu(features)
    fill = jnp.zeros((hpack.shape[2] - cols, part), f32)
    for j in range(n_lon):
        piece = act[:, lanes(j)]
        apack[j] = pack(piece, half).astype(bf16)
        hpack[0, j] = jnp.concatenate([piece[cells - cols:], fill], axis=0).astype(bf16)
        hpack[1, j] = jnp.concatenate([piece[:cols], fill], axis=0).astype(bf16)
    pl.semaphore_wait(barrier, greeted)
    for slot in (1, 0):
        weights[0, slot][1].start()
    exchange_one()
    assemble_one()

    weights_here(0, 1)
    for g, (_, _, offset, size) in enumerate(bands):
        total = multiply(0, 1, g)
        for j in range(n_lon):
            ysend1[j, offset:offset + size] = pack(total[:, lanes(j)], size).astype(bf16)
        for k in order:
            far_copy(0, g, k).start()
    weights_here(0, 0)
    for g, (_, _, offset, size) in enumerate(bands):
        total = multiply(0, 0, g)
        for j in range(n_lon):
            own[j, offset:offset + size] = pack(total[:, lanes(j)], size)
    for slot in (1, 0):
        weights[1, slot][1].start()
    for g, (_, _, offset, size) in enumerate(bands):
        for k in order:
            far_copy(0, g, k).wait_recv()
            slot = (lon + k) % n_lon
            value = own[slot, offset:offset + size] + yrecv1[slot, offset:offset + size].astype(f32)
            if k:
                zsend1[k, offset:offset + size] = value.astype(bf16)
                along_copy(0, g, k).start()
            else:
                kept[offset:offset + size] = value
    bias = b1_ref[:, lanes(0)]
    for j in away:
        bias = jnp.where(lon == j, b1_ref[:, lanes(j)], bias)
    bias = jnp.concatenate([bias, bias], axis=1)
    for g, (_, _, offset, size) in enumerate(bands):
        hidden = kept[offset:offset + size]
        for k in away:
            along_copy(0, g, k).wait_recv()
            hidden = hidden + zrecv1[k, offset:offset + size].astype(f32)
        hand_on(g, silu(hidden + bias))
    assemble_two()

    def chunk(slot, g, k):
        first, count = blocks[g][:2]
        start = pl.multiple_of(((lon + k) % n_lon) * cols, 8)
        return acc[slot, first:first + count, pl.ds(start, cols), :].reshape(count * cols, width)

    def padded(value, size):
        if size > value.shape[0]:
            value = jnp.concatenate([value, jnp.zeros((size - value.shape[0], width), f32)], axis=0)
        return value.astype(bf16)

    for slot in (1, 0):
        weights_here(1, slot)
        for g, (first, count, offset, size) in enumerate(blocks):
            acc[slot, first:first + count] = multiply(1, slot, g).reshape(count, all_cols, width)
            if slot:
                for k in order:
                    ysend2[(lon + k) % n_lon, offset:offset + size] = padded(chunk(1, g, k), size)
                    far_copy(1, g, k).start()
    for g, (first, count, offset, size) in enumerate(blocks):
        for k in order:
            far_copy(1, g, k).wait_recv()
            other = yrecv2[(lon + k) % n_lon, offset:offset + size].astype(f32)
            value = chunk(0, g, k) + other[:count * cols]
            if k:
                zsend2[k, offset:offset + size] = padded(value, size)
                along_copy(1, g, k).start()
            else:
                out_ref[0, first:first + count] = (value + b2_ref[...]).reshape(count, cols, width)
    for g, (first, count, offset, size) in enumerate(blocks):
        second = out_ref[0, first:first + count].reshape(count * cols, width)
        for k in away:
            along_copy(1, g, k).wait_recv()
            second = second + zrecv2[k, offset:offset + size].astype(f32)[:count * cols]
        out_ref[0, first:first + count] = second.reshape(count, cols, width)

    for k in order:
        forward_copy(k).wait_send()
        if k:
            main_copy(k).wait_send()
    for g in (0, 1):
        band_copy(g).wait_send()
    for side in (0, 1):
        @pl.when(sends[side])
        def _():
            for k in order:
                halo_copy(side, k).wait_send()
            for p in (0, 1):
                edge_copy(side, p).wait_send()

        @pl.when(gets[side])
        def _():
            halo_forward(side).wait_send()
    for conv in (0, 1):
        for slot in (0, 1):
            weights[conv, slot][1].wait_send()
        for g in (0, 1):
            for k in order:
                far_copy(conv, g, k).wait_send()
                if k:
                    along_copy(conv, g, k).wait_send()


def body(n_lat, n_lon, features, kernel_one, bias_one, kernel_two, bias_two):
    _, rows, cols, width = features.shape
    cells, part, all_cols = rows * cols, width // n_lon, cols * n_lon
    half = round_up(-(-cells // 2), 16)
    band_half, tall = row_groups(rows, all_cols, 2)[1], row_groups(rows, cols, 1)[1]
    short = round_up(cols, 16)
    bf16, f32 = jnp.bfloat16, jnp.float32
    dma = pltpu.SemaphoreType.DMA
    vmem = pl.BlockSpec(memory_space=pltpu.VMEM)
    anywhere = pl.BlockSpec(memory_space=pl.ANY)
    second = pl.pallas_call(
        functools.partial(block_kernel, n_lat, n_lon),
        out_shape=jax.ShapeDtypeStruct(features.shape, f32),
        in_specs=[vmem, anywhere, vmem, anywhere, vmem],
        out_specs=vmem,
        scratch_shapes=[
            pltpu.VMEM((2, 2, 3, 3, 2, part, width), bf16),
            pltpu.VMEM((n_lon, half, 2 * part), bf16),
            pltpu.VMEM((2, n_lon, half, 2 * part), bf16),
            pltpu.VMEM((2, n_lon, short, part), bf16),
            pltpu.VMEM((2, 2, n_lon, short, part), bf16),
            pltpu.VMEM((band_half, 2 * part), bf16),
            pltpu.VMEM((band_half, 2 * part), bf16),
            pltpu.VMEM((2, all_cols, part), bf16),
            pltpu.VMEM((2, 2, all_cols, part), bf16),
            pltpu.VMEM((rows + 2, all_cols + 2 * EDGE, 2 * part), f32),
            pltpu.VMEM((rows + 2, all_cols, 6 * part), bf16),
            pltpu.VMEM((n_lon, band_half, 2 * part), f32),
            pltpu.VMEM((band_half, 2 * part), f32),
            pltpu.VMEM((n_lon, band_half, 2 * part), bf16),
            pltpu.VMEM((n_lon, band_half, 2 * part), bf16),
            pltpu.VMEM((n_lon, band_half, 2 * part), bf16),
            pltpu.VMEM((n_lon, band_half, 2 * part), bf16),
            pltpu.VMEM((2, rows, all_cols, width), f32),
            pltpu.VMEM((n_lon, tall, width), bf16),
            pltpu.VMEM((n_lon, tall, width), bf16),
            pltpu.VMEM((n_lon, tall, width), bf16),
            pltpu.VMEM((n_lon, tall, width), bf16),
            dma((2, 2)), dma((2, 2)), dma((2, 2)),
            dma((2, n_lon)), dma((2, n_lon)),
            dma((2, n_lon)), dma((2, n_lon)), dma((2,)), dma((2,)),
            dma((2,)), dma((2,)), dma((2, 2)), dma((2, 2)),
            dma((2, 2, n_lon)), dma((2, 2, n_lon)), dma((2, 2, n_lon)), dma((2, 2, n_lon)),
        ],
        compiler_params=pltpu.CompilerParams(
            collective_id=0, has_side_effects=True, vmem_limit_bytes=56 * 2**20
        ),
        name="residual_block",
    )(features, kernel_one, bias_one.reshape(1, width), kernel_two, bias_two.reshape(1, width))
    return ((features.astype(f32) + second) * skip_scale).astype(bf16)


def solution(mesh):
    placed = (
        P(None, "lat", "lon", "ch"),
        P(None, None, "ch", "lon", None),
        P("ch"),
        P(None, None, "ch", "lon", None),
        P("ch"),
    )
    return jax.shard_map(
        functools.partial(body, mesh.shape["lat"], mesh.shape["lon"]),
        mesh=mesh, in_specs=placed, out_specs=P(None, "lat", "lon", "ch"), check_vma=False,
    )
```

```python
import functools

import jax
import jax.numpy as jnp
from jax import lax
from jax.experimental import pallas as pl
from jax.experimental.pallas import tpu as pltpu
from jax.sharding import PartitionSpec as P

skip_scale = 0.7071067811865476
MESH = pl.DeviceIdType.MESH
EDGE = 8


def round_up(value, step):
    return -(-value // step) * step


def silu(value):
    return value / (1.0 + jnp.exp(-value))


def pack(value, half):
    count, part = value.shape
    lower = value[half:]
    if 2 * half > count:
        lower = jnp.concatenate([lower, jnp.zeros((2 * half - count, part), value.dtype)], axis=0)
    return jnp.concatenate([value[:half], lower], axis=1)


def unpack(block, count):
    half, part = block.shape[0], block.shape[1] // 2
    return jnp.concatenate([block[:, :part], block[:count - half, part:]], axis=0)


def row_groups(counts, per_row, packed):
    groups, offset = [], 0
    for count in counts:
        size = round_up(-(-count * per_row // packed), 16)
        groups.append((count, offset, size))
        offset += size
    return groups, offset


def row_counts(rows):
    ahead = -(-rows // 2)
    return (ahead, rows - ahead), (ahead - 1, rows - ahead + 1)


def block_kernel(
    n_lat, n_lon, x_ref, k1_ref, b1_ref, k2_ref, b2_ref, out_ref,
    w, apack, arecv, hpack, hrecv, bpack, brecv, epack, erecv, field, taps,
    own, kept, ysend1, yrecv1, zsend1, zrecv1, acc, ysend2, yrecv2, zsend2, zrecv2,
    wl_sem, ws_sem, wr_sem, as_sem, ar_sem, hs_sem, hr_sem, fs_sem, fr_sem,
    bs_sem, br_sem, es_sem, er_sem, ys_sem, yr_sem, zs_sem, zr_sem,
):
    rows, cols, width = x_ref.shape[1:]
    cells = rows * cols
    part = width // n_lon
    half = apack.shape[1]
    all_cols = cols * n_lon
    counts = row_counts(rows)
    bands = row_groups(counts[0], all_cols, 2)[0]
    blocks = row_groups(counts[1], cols, 1)[0]
    f32, bf16 = jnp.float32, jnp.bfloat16
    lat, lon, ch = lax.axis_index("lat"), lax.axis_index("lon"), lax.axis_index("ch")
    flip = lat >= n_lat - n_lat // 2
    near = ch + 1 - 2 * (ch % 2)
    far = ch + 2 - 4 * ((ch // 2) % 2)
    near_far = near + 2 - 4 * ((near // 2) % 2)
    away = list(range(1, n_lon))
    order = away + [0]

    def device(up, along, channel):
        return {"lat": (lat + up) % n_lat, "lon": (lon + along) % n_lon, "ch": channel}

    def remote(src, dst, send, recv, target):
        return pltpu.make_async_remote_copy(
            src_ref=src, dst_ref=dst, send_sem=send, recv_sem=recv,
            device_id=target, device_id_type=MESH,
        )

    def weight_copies(conv, slot):
        source = (k1_ref, k2_ref)[conv]
        mine, theirs = ((ch, near), (far, near_far))[slot]

        def outputs(group):
            return source.at[:, :, 0, :, pl.ds(pl.multiple_of(group * width, width), width)]

        return (
            pltpu.make_async_copy(outputs(mine), w.at[conv, slot, :, :, 0], wl_sem.at[conv, slot]),
            remote(
                outputs(theirs), w.at[conv, slot, :, :, 1],
                ws_sem.at[conv, slot], wr_sem.at[conv, slot], device(0, 0, near),
            ),
        )

    weights = {(conv, slot): weight_copies(conv, slot) for conv in (0, 1) for slot in (1, 0)}
    for local, _ in weights.values():
        local.start()

    barrier = pltpu.get_barrier_semaphore()
    greeted = 0
    ups = sorted({0, 1, n_lat - 1})
    peers = [(up, along, ch) for up in ups for along in range(n_lon) if up or along]
    peers += [(up, 0, near) for up in ups] + [(0, 0, far)]
    for peer in peers:
        pl.semaphore_signal(barrier, inc=1, device_id=device(*peer), device_id_type=MESH)
        greeted += 1

    sends = (lat < n_lat - 1, lat > 0)
    gets = (lat > 0, lat < n_lat - 1)

    def main_copy(k):
        return remote(
            apack.at[(lon + k) % n_lon], arecv.at[0, k], as_sem.at[0, k], ar_sem.at[0, k], device(0, k, ch)
        )

    def forward_copy(k):
        return remote(
            arecv.at[0, k] if k else apack.at[lon], arecv.at[1, k],
            as_sem.at[1, k], ar_sem.at[1, k], device(0, 0, near),
        )

    def halo_copy(side, k):
        return remote(
            hpack.at[side, (lon + k) % n_lon], hrecv.at[side, 0, k],
            hs_sem.at[side, k], hr_sem.at[side, k], device((1, -1)[side] % n_lat, k, ch),
        )

    def halo_forward(side):
        return remote(
            hrecv.at[side, 0], hrecv.at[side, 1], fs_sem.at[side], fr_sem.at[side], device(0, 0, near)
        )

    def band_copy(g):
        place = pl.ds(*bands[g][1:])
        return remote(bpack.at[place], brecv.at[place], bs_sem.at[g], br_sem.at[g], device(0, 0, near))

    def edge_copy(side, p):
        return remote(
            epack.at[side], erecv.at[side, p], es_sem.at[side, p], er_sem.at[side, p],
            device((1, -1)[side] % n_lat, 0, (ch, near)[p]),
        )

    def piece_of(conv, g):
        return pl.ds(*(bands, blocks)[conv][g][1:])

    def far_copy(conv, g, k):
        src, dst = ((ysend1, yrecv1), (ysend2, yrecv2))[conv]
        slot, piece = (lon + k) % n_lon, piece_of(conv, g)
        return remote(
            src.at[slot, piece], dst.at[slot, piece],
            ys_sem.at[conv, g, k], yr_sem.at[conv, g, k], device(0, 0, far),
        )

    def along_copy(conv, g, k):
        src, dst = ((zsend1, zrecv1), (zsend2, zrecv2))[conv]
        piece = piece_of(conv, g)
        return remote(
            src.at[k, piece], dst.at[k, piece],
            zs_sem.at[conv, g, k], zr_sem.at[conv, g, k], device(0, k, ch),
        )

    def first_row(conv, g):
        ahead, behind = counts[conv]
        return jnp.where(flip, (behind, 0)[g], (0, ahead)[g])

    def lanes(p):
        return slice(p * part, (p + 1) * part)

    inside = slice(EDGE, EDGE + all_cols)

    def fold(side):
        row, inner = ((0, 1), (rows + 1, rows))[side]
        turn = all_cols // 2
        field[row, EDGE:EDGE + turn] = field[inner, EDGE + turn:EDGE + all_cols]
        field[row, EDGE + turn:EDGE + all_cols] = field[inner, EDGE:EDGE + turn]

    def spread(first, count):
        here = pl.ds(first, count)
        field[here, EDGE - 1:EDGE] = field[here, EDGE + all_cols - 1:EDGE + all_cols]
        field[here, EDGE + all_cols:EDGE + all_cols + 1] = field[here, EDGE:EDGE + 1]
        for e in range(3):
            taps[here, :, e * 2 * part:(e + 1) * 2 * part] = field[
                here, EDGE - 1 + e:EDGE - 1 + e + all_cols
            ].astype(bf16)

    def exchange_one():
        for k in away:
            main_copy(k).start()
        for side in (0, 1):
            @pl.when(sends[side])
            def _():
                for k in order:
                    halo_copy(side, k).start()
        forward_copy(0).start()

    def assemble_one():
        def place(k):
            return pl.ds(pl.multiple_of(EDGE + ((lon - k + n_lon) % n_lon) * cols, 8), cols)

        def cell_block(block):
            return unpack(block.astype(f32), cells).reshape(rows, cols, part)

        field[1:rows + 1, place(0), lanes(0)] = cell_block(apack[lon])
        for k in away:
            main_copy(k).wait_recv()
            forward_copy(k).start()
            field[1:rows + 1, place(k), lanes(0)] = cell_block(arecv[0, k])
        for side in (0, 1):
            @pl.when(gets[side])
            def _():
                for k in order:
                    halo_copy(side, k).wait_recv()
                halo_forward(side).start()
        for k in [0] + away:
            forward_copy(k).wait_recv()
            field[1:rows + 1, place(k), lanes(1)] = cell_block(arecv[1, k])
        for side in (0, 1):
            @pl.when(gets[side])
            def _():
                halo_forward(side).wait_recv()
                for p in (0, 1):
                    for k in order:
                        field[(0, rows + 1)[side], place(k), lanes(p)] = hrecv[side, p, k].astype(f32)[:cols]

            @pl.when(jnp.logical_not(gets[side]))
            def _():
                fold(side)
        spread(0, rows + 2)

    def hand_on(g, act):
        count, offset, size = bands[g]
        bpack[offset:offset + size] = act.astype(bf16)
        band_copy(g).start()
        band = unpack(act, count * all_cols)
        for side in (0, 1):
            turned = flip if side == g else jnp.logical_not(flip)

            @pl.when(jnp.logical_and(sends[side], turned))
            def _():
                epack[side] = (band[-all_cols:], band[:all_cols])[side].astype(bf16)
                for p in (1, 0):
                    edge_copy(side, p).start()
        field[pl.ds(first_row(0, g) + 1, count), inside, lanes(0)] = band.reshape(count, all_cols, part)

    def assemble_two(g):
        count, offset, size = bands[g]
        band_copy(g).wait_recv()
        other = unpack(brecv[offset:offset + size].astype(f32), count * all_cols)
        field[pl.ds(first_row(0, g) + 1, count), inside, lanes(1)] = other.reshape(count, all_cols, part)
        for side in (0, 1):
            due = jnp.logical_not(flip) if side == g else flip

            @pl.when(jnp.logical_and(gets[side], due))
            def _():
                for p in (0, 1):
                    edge_copy(side, p).wait_recv()
                    field[(0, rows + 1)[side], inside, lanes(p)] = erecv[side, p].astype(f32)

            @pl.when(jnp.logical_and(jnp.logical_not(gets[side]), due))
            def _():
                fold(side)
        count += 1
        spread(jnp.where(flip, (rows + 2 - count, 0)[g], (0, rows + 2 - count)[g]), count)

    def weights_here(conv, slot):
        local, other = weights[conv, slot]
        local.wait()
        other.wait_recv()

    def multiply(conv, slot, g):
        first, count = first_row(conv, g), counts[conv][g]
        total = None
        for a in range(3):
            term = jnp.dot(
                taps[pl.ds(first + a, count)].reshape(count * all_cols, 6 * part),
                w[conv, slot, a].reshape(6 * part, width),
                preferred_element_type=f32,
            )
            total = term if total is None else total + term
        return total

    features = x_ref[0].astype(f32).reshape(cells, width)
    act = silu(features)
    fill = jnp.zeros((hpack.shape[2] - cols, part), f32)
    for j in range(n_lon):
        piece = act[:, lanes(j)]
        apack[j] = pack(piece, half).astype(bf16)
        hpack[0, j] = jnp.concatenate([piece[cells - cols:], fill], axis=0).astype(bf16)
        hpack[1, j] = jnp.concatenate([piece[:cols], fill], axis=0).astype(bf16)
    pl.semaphore_wait(barrier, greeted)
    for slot in (1, 0):
        weights[0, slot][1].start()
    exchange_one()
    assemble_one()

    weights_here(0, 1)
    for g, (_, offset, size) in enumerate(bands):
        total = multiply(0, 1, g)
        for j in range(n_lon):
            ysend1[j, offset:offset + size] = pack(total[:, lanes(j)], size).astype(bf16)
        for k in order:
            far_copy(0, g, k).start()
    weights_here(0, 0)
    for g, (_, offset, size) in enumerate(bands):
        total = multiply(0, 0, g)
        for j in range(n_lon):
            own[j, offset:offset + size] = pack(total[:, lanes(j)], size)
    for slot in (1, 0):
        weights[1, slot][1].start()
    for g, (_, offset, size) in enumerate(bands):
        for k in order:
            far_copy(0, g, k).wait_recv()
            slot = (lon + k) % n_lon
            value = own[slot, offset:offset + size] + yrecv1[slot, offset:offset + size].astype(f32)
            if k:
                zsend1[k, offset:offset + size] = value.astype(bf16)
                along_copy(0, g, k).start()
            else:
                kept[offset:offset + size] = value
    bias = b1_ref[:, lanes(0)]
    for j in away:
        bias = jnp.where(lon == j, b1_ref[:, lanes(j)], bias)
    bias = jnp.concatenate([bias, bias], axis=1)

    def chunk(slot, g, k):
        count = counts[1][g]
        start = pl.multiple_of(((lon + k) % n_lon) * cols, 8)
        return acc[slot, pl.ds(first_row(1, g), count), pl.ds(start, cols), :].reshape(count * cols, width)

    def padded(value, size):
        if size > value.shape[0]:
            value = jnp.concatenate([value, jnp.zeros((size - value.shape[0], width), f32)], axis=0)
        return value.astype(bf16)

    def multiply_two(slot, g):
        count, offset, size = blocks[g]
        acc[slot, pl.ds(first_row(1, g), count)] = multiply(1, slot, g).reshape(count, all_cols, width)
        if slot:
            for k in order:
                ysend2[(lon + k) % n_lon, offset:offset + size] = padded(chunk(1, g, k), size)
                far_copy(1, g, k).start()

    def gather_one(g):
        _, offset, size = bands[g]
        hidden = kept[offset:offset + size]
        for k in away:
            along_copy(0, g, k).wait_recv()
            hidden = hidden + zrecv1[k, offset:offset + size].astype(f32)
        hand_on(g, silu(hidden + bias))

    def scatter_two(g):
        count, offset, size = blocks[g]
        for k in order:
            far_copy(1, g, k).wait_recv()
            other = yrecv2[(lon + k) % n_lon, offset:offset + size].astype(f32)
            value = chunk(0, g, k) + other[:count * cols]
            if k:
                zsend2[k, offset:offset + size] = padded(value, size)
                along_copy(1, g, k).start()
            else:
                out_ref[0, pl.ds(first_row(1, g), count)] = (value + b2_ref[...]).reshape(count, cols, width)

    gather_one(0)
    assemble_two(0)
    weights_here(1, 1)
    multiply_two(1, 0)
    gather_one(1)
    weights_here(1, 0)
    multiply_two(0, 0)
    assemble_two(1)
    multiply_two(1, 1)
    scatter_two(0)
    multiply_two(0, 1)
    scatter_two(1)
    for g, (count, offset, size) in enumerate(blocks):
        here = pl.ds(first_row(1, g), count)
        second = out_ref[0, here].reshape(count * cols, width)
        for k in away:
            along_copy(1, g, k).wait_recv()
            second = second + zrecv2[k, offset:offset + size].astype(f32)[:count * cols]
        out_ref[0, here] = second.reshape(count, cols, width)

    for k in order:
        forward_copy(k).wait_send()
        if k:
            main_copy(k).wait_send()
    for g in (0, 1):
        band_copy(g).wait_send()
    for side in (0, 1):
        @pl.when(sends[side])
        def _():
            for k in order:
                halo_copy(side, k).wait_send()
            for p in (0, 1):
                edge_copy(side, p).wait_send()

        @pl.when(gets[side])
        def _():
            halo_forward(side).wait_send()
    for conv in (0, 1):
        for slot in (0, 1):
            weights[conv, slot][1].wait_send()
        for g in (0, 1):
            for k in order:
                far_copy(conv, g, k).wait_send()
                if k:
                    along_copy(conv, g, k).wait_send()


def body(n_lat, n_lon, features, kernel_one, bias_one, kernel_two, bias_two):
    _, rows, cols, width = features.shape
    cells, part, all_cols = rows * cols, width // n_lon, cols * n_lon
    half = round_up(-(-cells // 2), 16)
    counts = row_counts(rows)
    band_half, tall = row_groups(counts[0], all_cols, 2)[1], row_groups(counts[1], cols, 1)[1]
    short = round_up(cols, 16)
    bf16, f32 = jnp.bfloat16, jnp.float32
    dma = pltpu.SemaphoreType.DMA
    vmem = pl.BlockSpec(memory_space=pltpu.VMEM)
    anywhere = pl.BlockSpec(memory_space=pl.ANY)
    second = pl.pallas_call(
        functools.partial(block_kernel, n_lat, n_lon),
        out_shape=jax.ShapeDtypeStruct(features.shape, f32),
        in_specs=[vmem, anywhere, vmem, anywhere, vmem],
        out_specs=vmem,
        scratch_shapes=[
            pltpu.VMEM((2, 2, 3, 3, 2, part, width), bf16),
            pltpu.VMEM((n_lon, half, 2 * part), bf16),
            pltpu.VMEM((2, n_lon, half, 2 * part), bf16),
            pltpu.VMEM((2, n_lon, short, part), bf16),
            pltpu.VMEM((2, 2, n_lon, short, part), bf16),
            pltpu.VMEM((band_half, 2 * part), bf16),
            pltpu.VMEM((band_half, 2 * part), bf16),
            pltpu.VMEM((2, all_cols, part), bf16),
            pltpu.VMEM((2, 2, all_cols, part), bf16),
            pltpu.VMEM((rows + 2, all_cols + 2 * EDGE, 2 * part), f32),
            pltpu.VMEM((rows + 2, all_cols, 6 * part), bf16),
            pltpu.VMEM((n_lon, band_half, 2 * part), f32),
            pltpu.VMEM((band_half, 2 * part), f32),
            pltpu.VMEM((n_lon, band_half, 2 * part), bf16),
            pltpu.VMEM((n_lon, band_half, 2 * part), bf16),
            pltpu.VMEM((n_lon, band_half, 2 * part), bf16),
            pltpu.VMEM((n_lon, band_half, 2 * part), bf16),
            pltpu.VMEM((2, rows, all_cols, width), f32),
            pltpu.VMEM((n_lon, tall, width), bf16),
            pltpu.VMEM((n_lon, tall, width), bf16),
            pltpu.VMEM((n_lon, tall, width), bf16),
            pltpu.VMEM((n_lon, tall, width), bf16),
            dma((2, 2)), dma((2, 2)), dma((2, 2)),
            dma((2, n_lon)), dma((2, n_lon)),
            dma((2, n_lon)), dma((2, n_lon)), dma((2,)), dma((2,)),
            dma((2,)), dma((2,)), dma((2, 2)), dma((2, 2)),
            dma((2, 2, n_lon)), dma((2, 2, n_lon)), dma((2, 2, n_lon)), dma((2, 2, n_lon)),
        ],
        compiler_params=pltpu.CompilerParams(
            collective_id=0, has_side_effects=True, vmem_limit_bytes=56 * 2**20
        ),
        name="residual_block",
    )(features, kernel_one, bias_one.reshape(1, width), kernel_two, bias_two.reshape(1, width))
    return ((features.astype(f32) + second) * skip_scale).astype(bf16)


def solution(mesh):
    placed = (
        P(None, "lat", "lon", "ch"),
        P(None, None, "ch", "lon", None),
        P("ch"),
        P(None, None, "ch", "lon", None),
        P("ch"),
    )
    return jax.shard_map(
        functools.partial(body, mesh.shape["lat"], mesh.shape["lon"]),
        mesh=mesh, in_specs=placed, out_specs=P(None, "lat", "lon", "ch"), check_vma=False,
    )
```

```python
import functools

import jax
import jax.numpy as jnp
from jax import lax
from jax.experimental import pallas as pl
from jax.experimental.pallas import tpu as pltpu
from jax.sharding import PartitionSpec as P

skip_scale = 0.7071067811865476
MESH = pl.DeviceIdType.MESH
EDGE = 8


def round_up(value, step):
    return -(-value // step) * step


def silu(value):
    return value / (1.0 + jnp.exp(-value))


def pack(value, half):
    count, part = value.shape
    lower = value[half:]
    if 2 * half > count:
        lower = jnp.concatenate([lower, jnp.zeros((2 * half - count, part), value.dtype)], axis=0)
    return jnp.concatenate([value[:half], lower], axis=1)


def unpack(block, count):
    half, part = block.shape[0], block.shape[1] // 2
    return jnp.concatenate([block[:, :part], block[:count - half, part:]], axis=0)


def row_groups(counts, per_row, packed):
    groups, offset = [], 0
    for count in counts:
        size = round_up(-(-count * per_row // packed), 16)
        groups.append((count, offset, size))
        offset += size
    return groups, offset


def row_counts(rows):
    ahead = -(-rows // 2)
    return (ahead, rows - ahead), (ahead - 1, rows - ahead + 1)


def block_kernel(
    n_lat, n_lon, x_ref, k1_ref, b1_ref, k2_ref, b2_ref, out_ref,
    x_vmem, b1_vmem, b2_vmem, w, apack, arecv, bpack, brecv, epack, erecv, field, taps,
    own, kept, ysend1, yrecv1, zsend1, zrecv1, acc, ysend2, yrecv2, zsend2, zrecv2,
    in_sem, wl_sem, ws_sem, wr_sem, as_sem, ar_sem,
    bs_sem, br_sem, es_sem, er_sem, ys_sem, yr_sem, zs_sem, zr_sem,
):
    rows, cols, width = x_ref.shape[1:]
    cells = rows * cols
    part = width // n_lon
    half = apack.shape[1]
    all_cols = cols * n_lon
    counts = row_counts(rows)
    bands = row_groups(counts[0], all_cols, 2)[0]
    blocks = row_groups(counts[1], cols, 1)[0]
    f32, bf16 = jnp.float32, jnp.bfloat16
    lat, lon, ch = lax.axis_index("lat"), lax.axis_index("lon"), lax.axis_index("ch")
    flip = lat >= n_lat - n_lat // 2
    near = ch + 1 - 2 * (ch % 2)
    far = ch + 2 - 4 * ((ch // 2) % 2)
    near_far = near + 2 - 4 * ((near // 2) % 2)
    away = list(range(1, n_lon))
    order = away + [0]

    def device(up, along, channel):
        return {"lat": (lat + up) % n_lat, "lon": (lon + along) % n_lon, "ch": channel}

    def remote(src, dst, send, recv, target):
        return pltpu.make_async_remote_copy(
            src_ref=src, dst_ref=dst, send_sem=send, recv_sem=recv,
            device_id=target, device_id_type=MESH,
        )

    def weight_copies(conv, slot):
        source = (k1_ref, k2_ref)[conv]
        mine, theirs = ((ch, near), (far, near_far))[slot]

        def outputs(group):
            return source.at[:, :, 0, :, pl.ds(pl.multiple_of(group * width, width), width)]

        return (
            pltpu.make_async_copy(outputs(mine), w.at[conv, slot, :, :, 0], wl_sem.at[conv, slot]),
            remote(
                outputs(theirs), w.at[conv, slot, :, :, 1],
                ws_sem.at[conv, slot], wr_sem.at[conv, slot], device(0, 0, near),
            ),
        )

    barrier = pltpu.get_barrier_semaphore()
    greeted = 0
    peers = [(0, along, ch) for along in away] + [(0, 0, near), (0, 0, far)]
    peers += [(up, 0, channel) for up in sorted({1, n_lat - 1}) for channel in (ch, near)]
    for peer in peers:
        pl.semaphore_signal(barrier, inc=1, device_id=device(*peer), device_id_type=MESH)
        greeted += 1

    inputs = [
        pltpu.make_async_copy(src, dst, in_sem.at[i])
        for i, (src, dst) in enumerate(((x_ref, x_vmem), (b1_ref, b1_vmem), (b2_ref, b2_vmem)))
    ]
    for copy in inputs:
        copy.start()
    weights = {(conv, slot): weight_copies(conv, slot) for conv in (0, 1) for slot in (1, 0)}
    for local, _ in weights.values():
        local.start()

    sends = (lat < n_lat - 1, lat > 0)
    gets = (lat > 0, lat < n_lat - 1)

    def main_copy(k):
        return remote(
            apack.at[(lon + k) % n_lon], arecv.at[0, k], as_sem.at[0, k], ar_sem.at[0, k], device(0, k, ch)
        )

    def forward_copy(k):
        return remote(
            arecv.at[0, k] if k else apack.at[lon], arecv.at[1, k],
            as_sem.at[1, k], ar_sem.at[1, k], device(0, 0, near),
        )

    def band_copy(g):
        place = pl.ds(*bands[g][1:])
        return remote(bpack.at[place], brecv.at[place], bs_sem.at[g], br_sem.at[g], device(0, 0, near))

    def edge_copy(conv, side, p):
        return remote(
            epack.at[conv, side], erecv.at[conv, side, p], es_sem.at[conv, side, p], er_sem.at[conv, side, p],
            device((1, -1)[side] % n_lat, 0, (ch, near)[p]),
        )

    def piece_of(conv, g):
        return pl.ds(*(bands, blocks)[conv][g][1:])

    def far_copy(conv, g, k):
        src, dst = ((ysend1, yrecv1), (ysend2, yrecv2))[conv]
        slot, piece = (lon + k) % n_lon, piece_of(conv, g)
        return remote(
            src.at[slot, piece], dst.at[slot, piece],
            ys_sem.at[conv, g, k], yr_sem.at[conv, g, k], device(0, 0, far),
        )

    def along_copy(conv, g, k):
        src, dst = ((zsend1, zrecv1), (zsend2, zrecv2))[conv]
        piece = piece_of(conv, g)
        return remote(
            src.at[k, piece], dst.at[k, piece],
            zs_sem.at[conv, g, k], zr_sem.at[conv, g, k], device(0, k, ch),
        )

    def first_row(conv, g):
        ahead, behind = counts[conv]
        return jnp.where(flip, (behind, 0)[g], (0, ahead)[g])

    def lanes(p):
        return slice(p * part, (p + 1) * part)

    inside = slice(EDGE, EDGE + all_cols)

    def send_edge(conv, side, edge, due=True):
        @pl.when(jnp.logical_and(sends[side], due))
        def _():
            epack[conv, side] = edge.astype(bf16)
            for p in (1, 0):
                edge_copy(conv, side, p).start()

    def close(conv, g):
        for side in (0, 1):
            due = jnp.logical_not(flip) if side == g else flip
            row, inner = ((0, 1), (rows + 1, rows))[side]

            @pl.when(jnp.logical_and(gets[side], due))
            def _():
                for p in (0, 1):
                    edge_copy(conv, side, p).wait_recv()
                    field[row, inside, lanes(p)] = erecv[conv, side, p].astype(f32)

            @pl.when(jnp.logical_and(jnp.logical_not(gets[side]), due))
            def _():
                turn = all_cols // 2
                field[row, EDGE:EDGE + turn] = field[inner, EDGE + turn:EDGE + all_cols]
                field[row, EDGE + turn:EDGE + all_cols] = field[inner, EDGE:EDGE + turn]

        ahead = counts[conv][0] + 2
        behind = rows + 2 - ahead
        here = pl.ds(jnp.where(flip, (behind, 0)[g], (0, ahead)[g]), (ahead, behind)[g])
        field[here, EDGE - 1:EDGE] = field[here, EDGE + all_cols - 1:EDGE + all_cols]
        field[here, EDGE + all_cols:EDGE + all_cols + 1] = field[here, EDGE:EDGE + 1]
        for e in range(3):
            taps[here, :, e * 2 * part:(e + 1) * 2 * part] = field[
                here, EDGE - 1 + e:EDGE - 1 + e + all_cols
            ].astype(bf16)

    def exchange_one():
        for k in away:
            main_copy(k).start()
        forward_copy(0).start()

    def assemble_one():
        def place(k):
            return pl.ds(pl.multiple_of(EDGE + ((lon - k + n_lon) % n_lon) * cols, 8), cols)

        def cell_block(block):
            return unpack(block.astype(f32), cells).reshape(rows, cols, part)

        field[1:rows + 1, place(0), lanes(0)] = cell_block(apack[lon])
        for k in away:
            main_copy(k).wait_recv()
            forward_copy(k).start()
            field[1:rows + 1, place(k), lanes(0)] = cell_block(arecv[0, k])
        weights[0, 0][1].start()
        for side in (0, 1):
            send_edge(0, side, field[(rows, 1)[side], inside, lanes(0)])
        for k in [0] + away:
            forward_copy(k).wait_recv()
            field[1:rows + 1, place(k), lanes(1)] = cell_block(arecv[1, k])

    def hand_on(g, act):
        count, offset, size = bands[g]
        bpack[offset:offset + size] = act.astype(bf16)
        band_copy(g).start()
        band = unpack(act, count * all_cols)
        for side in (0, 1):
            turned = flip if side == g else jnp.logical_not(flip)
            send_edge(1, side, (band[-all_cols:], band[:all_cols])[side], turned)
        field[pl.ds(first_row(0, g) + 1, count), inside, lanes(0)] = band.reshape(count, all_cols, part)

    def assemble_two(g):
        count, offset, size = bands[g]
        band_copy(g).wait_recv()
        other = unpack(brecv[offset:offset + size].astype(f32), count * all_cols)
        field[pl.ds(first_row(0, g) + 1, count), inside, lanes(1)] = other.reshape(count, all_cols, part)
        close(1, g)

    def weights_here(conv, slot):
        local, other = weights[conv, slot]
        local.wait()
        other.wait_recv()

    def multiply(conv, slot, g):
        first, count = first_row(conv, g), counts[conv][g]
        total = None
        for a in range(3):
            term = jnp.dot(
                taps[pl.ds(first + a, count)].reshape(count * all_cols, 6 * part),
                w[conv, slot, a].reshape(6 * part, width),
                preferred_element_type=f32,
            )
            total = term if total is None else total + term
        return total

    inputs[0].wait()
    act = silu(x_vmem[0].astype(f32).reshape(cells, width))
    for j in range(n_lon):
        apack[j] = pack(act[:, lanes(j)], half).astype(bf16)
    pl.semaphore_wait(barrier, greeted)
    weights[0, 1][1].start()
    exchange_one()
    assemble_one()

    for g, (_, offset, size) in enumerate(bands):
        close(0, g)
        if g == 0:
            weights_here(0, 1)
        total = multiply(0, 1, g)
        for j in range(n_lon):
            ysend1[j, offset:offset + size] = pack(total[:, lanes(j)], size).astype(bf16)
        for k in order:
            far_copy(0, g, k).start()
    weights_here(0, 0)
    for g, (_, offset, size) in enumerate(bands):
        total = multiply(0, 0, g)
        for j in range(n_lon):
            own[j, offset:offset + size] = pack(total[:, lanes(j)], size)
    for slot in (1, 0):
        weights[1, slot][1].start()
    for g, (_, offset, size) in enumerate(bands):
        for k in order:
            far_copy(0, g, k).wait_recv()
            slot = (lon + k) % n_lon
            value = own[slot, offset:offset + size] + yrecv1[slot, offset:offset + size].astype(f32)
            if k:
                zsend1[k, offset:offset + size] = value.astype(bf16)
                along_copy(0, g, k).start()
            else:
                kept[offset:offset + size] = value
    for copy in inputs[1:]:
        copy.wait()
    bias = b1_vmem[:, lanes(0)]
    for j in away:
        bias = jnp.where(lon == j, b1_vmem[:, lanes(j)], bias)
    bias = jnp.concatenate([bias, bias], axis=1)

    def chunk(slot, g, k):
        count = counts[1][g]
        start = pl.multiple_of(((lon + k) % n_lon) * cols, 8)
        return acc[slot, pl.ds(first_row(1, g), count), pl.ds(start, cols), :].reshape(count * cols, width)

    def padded(value, size):
        if size > value.shape[0]:
            value = jnp.concatenate([value, jnp.zeros((size - value.shape[0], width), f32)], axis=0)
        return value.astype(bf16)

    def multiply_two(slot, g):
        count, offset, size = blocks[g]
        acc[slot, pl.ds(first_row(1, g), count)] = multiply(1, slot, g).reshape(count, all_cols, width)
        if slot:
            for k in order:
                ysend2[(lon + k) % n_lon, offset:offset + size] = padded(chunk(1, g, k), size)
                far_copy(1, g, k).start()

    def gather_one(g):
        _, offset, size = bands[g]
        hidden = kept[offset:offset + size]
        for k in away:
            along_copy(0, g, k).wait_recv()
            hidden = hidden + zrecv1[k, offset:offset + size].astype(f32)
        hand_on(g, silu(hidden + bias))

    def scatter_two(g):
        count, offset, size = blocks[g]
        for k in order:
            far_copy(1, g, k).wait_recv()
            other = yrecv2[(lon + k) % n_lon, offset:offset + size].astype(f32)
            value = chunk(0, g, k) + other[:count * cols]
            if k:
                zsend2[k, offset:offset + size] = padded(value, size)
                along_copy(1, g, k).start()
            else:
                out_ref[0, pl.ds(first_row(1, g), count)] = (value + b2_vmem[...]).reshape(count, cols, width)

    gather_one(0)
    assemble_two(0)
    weights_here(1, 1)
    multiply_two(1, 0)
    gather_one(1)
    weights_here(1, 0)
    multiply_two(0, 0)
    assemble_two(1)
    multiply_two(1, 1)
    scatter_two(0)
    multiply_two(0, 1)
    scatter_two(1)
    for g, (count, offset, size) in enumerate(blocks):
        here = pl.ds(first_row(1, g), count)
        second = out_ref[0, here].reshape(count * cols, width)
        for k in away:
            along_copy(1, g, k).wait_recv()
            second = second + zrecv2[k, offset:offset + size].astype(f32)[:count * cols]
        out_ref[0, here] = second.reshape(count, cols, width)

    for k in order:
        forward_copy(k).wait_send()
        if k:
            main_copy(k).wait_send()
    for g in (0, 1):
        band_copy(g).wait_send()
    for conv in (0, 1):
        for side in (0, 1):
            @pl.when(sends[side])
            def _():
                for p in (0, 1):
                    edge_copy(conv, side, p).wait_send()
    for conv in (0, 1):
        for slot in (0, 1):
            weights[conv, slot][1].wait_send()
        for g in (0, 1):
            for k in order:
                far_copy(conv, g, k).wait_send()
                if k:
                    along_copy(conv, g, k).wait_send()


def body(n_lat, n_lon, features, kernel_one, bias_one, kernel_two, bias_two):
    _, rows, cols, width = features.shape
    cells, part, all_cols = rows * cols, width // n_lon, cols * n_lon
    half = round_up(-(-cells // 2), 16)
    counts = row_counts(rows)
    band_half, tall = row_groups(counts[0], all_cols, 2)[1], row_groups(counts[1], cols, 1)[1]
    bf16, f32 = jnp.bfloat16, jnp.float32
    dma = pltpu.SemaphoreType.DMA
    vmem = pl.BlockSpec(memory_space=pltpu.VMEM)
    anywhere = pl.BlockSpec(memory_space=pl.ANY)
    second = pl.pallas_call(
        functools.partial(block_kernel, n_lat, n_lon),
        out_shape=jax.ShapeDtypeStruct(features.shape, f32),
        in_specs=[anywhere] * 5,
        out_specs=vmem,
        scratch_shapes=[
            pltpu.VMEM(features.shape, bf16),
            pltpu.VMEM((1, width), f32),
            pltpu.VMEM((1, width), f32),
            pltpu.VMEM((2, 2, 3, 3, 2, part, width), bf16),
            pltpu.VMEM((n_lon, half, 2 * part), bf16),
            pltpu.VMEM((2, n_lon, half, 2 * part), bf16),
            pltpu.VMEM((band_half, 2 * part), bf16),
            pltpu.VMEM((band_half, 2 * part), bf16),
            pltpu.VMEM((2, 2, all_cols, part), bf16),
            pltpu.VMEM((2, 2, 2, all_cols, part), bf16),
            pltpu.VMEM((rows + 2, all_cols + 2 * EDGE, 2 * part), f32),
            pltpu.VMEM((rows + 2, all_cols, 6 * part), bf16),
            pltpu.VMEM((n_lon, band_half, 2 * part), f32),
            pltpu.VMEM((band_half, 2 * part), f32),
            pltpu.VMEM((n_lon, band_half, 2 * part), bf16),
            pltpu.VMEM((n_lon, band_half, 2 * part), bf16),
            pltpu.VMEM((n_lon, band_half, 2 * part), bf16),
            pltpu.VMEM((n_lon, band_half, 2 * part), bf16),
            pltpu.VMEM((2, rows, all_cols, width), f32),
            pltpu.VMEM((n_lon, tall, width), bf16),
            pltpu.VMEM((n_lon, tall, width), bf16),
            pltpu.VMEM((n_lon, tall, width), bf16),
            pltpu.VMEM((n_lon, tall, width), bf16),
            dma((3,)), dma((2, 2)), dma((2, 2)), dma((2, 2)),
            dma((2, n_lon)), dma((2, n_lon)),
            dma((2,)), dma((2,)), dma((2, 2, 2)), dma((2, 2, 2)),
            dma((2, 2, n_lon)), dma((2, 2, n_lon)), dma((2, 2, n_lon)), dma((2, 2, n_lon)),
        ],
        compiler_params=pltpu.CompilerParams(
            collective_id=0, has_side_effects=True, vmem_limit_bytes=56 * 2**20
        ),
        name="residual_block",
    )(features, kernel_one, bias_one.reshape(1, width), kernel_two, bias_two.reshape(1, width))
    return ((features.astype(f32) + second) * skip_scale).astype(bf16)


def solution(mesh):
    placed = (
        P(None, "lat", "lon", "ch"),
        P(None, None, "ch", "lon", None),
        P("ch"),
        P(None, None, "ch", "lon", None),
        P("ch"),
    )
    return jax.shard_map(
        functools.partial(body, mesh.shape["lat"], mesh.shape["lon"]),
        mesh=mesh, in_specs=placed, out_specs=P(None, "lat", "lon", "ch"), check_vma=False,
    )
```

```python
import functools

import jax
import jax.numpy as jnp
from jax import lax
from jax.experimental import pallas as pl
from jax.experimental.pallas import tpu as pltpu
from jax.sharding import PartitionSpec as P

skip_scale = 0.7071067811865476
MESH = pl.DeviceIdType.MESH
EDGE = 8


def round_up(value, step):
    return -(-value // step) * step


def silu(value):
    return value / (1.0 + jnp.exp(-value))


def pack(value, half):
    count, part = value.shape
    lower = value[half:]
    if 2 * half > count:
        lower = jnp.concatenate([lower, jnp.zeros((2 * half - count, part), value.dtype)], axis=0)
    return jnp.concatenate([value[:half], lower], axis=1)


def unpack(block, count):
    half, part = block.shape[0], block.shape[1] // 2
    return jnp.concatenate([block[:, :part], block[:count - half, part:]], axis=0)


def row_groups(counts, per_row, packed):
    groups, offset = [], 0
    for count in counts:
        size = round_up(-(-count * per_row // packed), 16)
        groups.append((count, offset, size))
        offset += size
    return groups, offset


def row_counts(rows):
    ahead = -(-rows // 2)
    return (ahead, rows - ahead), (ahead - 1, rows - ahead + 1)


def block_kernel(
    n_lat, n_lon, x_ref, k1_ref, b1_ref, k2_ref, b2_ref, out_ref,
    x_vmem, b1_vmem, b2_vmem, w, apack, arecv, bpack, brecv, epack, erecv, field, taps,
    own, kept, ysend1, yrecv1, zsend1, zrecv1, acc, ysend2, yrecv2, zsend2, zrecv2,
    in_sem, wl_sem, ws_sem, wr_sem, as_sem, ar_sem,
    bs_sem, br_sem, es_sem, er_sem, ys_sem, yr_sem, zs_sem, zr_sem,
):
    rows, cols, width = x_ref.shape[1:]
    cells = rows * cols
    part = width // n_lon
    half = apack.shape[1]
    all_cols = cols * n_lon
    counts = row_counts(rows)
    bands = row_groups(counts[0], all_cols, 2)[0]
    blocks = row_groups(counts[1], cols, 1)[0]
    f32, bf16 = jnp.float32, jnp.bfloat16
    lat, lon, ch = lax.axis_index("lat"), lax.axis_index("lon"), lax.axis_index("ch")
    flip = lat >= n_lat - n_lat // 2
    near = ch + 1 - 2 * (ch % 2)
    far = ch + 2 - 4 * ((ch // 2) % 2)
    near_far = near + 2 - 4 * ((near // 2) % 2)
    away = list(range(1, n_lon))
    order = away + [0]

    def device(up, along, channel):
        return {"lat": (lat + up) % n_lat, "lon": (lon + along) % n_lon, "ch": channel}

    def remote(src, dst, send, recv, target):
        return pltpu.make_async_remote_copy(
            src_ref=src, dst_ref=dst, send_sem=send, recv_sem=recv,
            device_id=target, device_id_type=MESH,
        )

    def weight_copies(conv, slot):
        source = (k1_ref, k2_ref)[conv]
        mine, theirs = ((ch, near), (far, near_far))[slot]

        def outputs(group):
            return source.at[:, :, 0, :, pl.ds(pl.multiple_of(group * width, width), width)]

        return (
            pltpu.make_async_copy(outputs(mine), w.at[conv, slot, :, :, 0], wl_sem.at[conv, slot]),
            remote(
                outputs(theirs), w.at[conv, slot, :, :, 1],
                ws_sem.at[conv, slot], wr_sem.at[conv, slot], device(0, 0, near),
            ),
        )

    barrier = pltpu.get_barrier_semaphore()
    greeted = 0
    peers = [(0, along, ch) for along in away] + [(0, 0, near), (0, 0, far)]
    peers += [(up, 0, channel) for up in sorted({1, n_lat - 1}) for channel in (ch, near)]
    for peer in peers:
        pl.semaphore_signal(barrier, inc=1, device_id=device(*peer), device_id_type=MESH)
        greeted += 1

    inputs = [
        pltpu.make_async_copy(src, dst, in_sem.at[i])
        for i, (src, dst) in enumerate(((x_ref, x_vmem), (b1_ref, b1_vmem), (b2_ref, b2_vmem)))
    ]
    for copy in inputs:
        copy.start()
    weights = {(conv, slot): weight_copies(conv, slot) for conv in (0, 1) for slot in (1, 0)}
    for local, _ in weights.values():
        local.start()

    sends = (lat < n_lat - 1, lat > 0)
    gets = (lat > 0, lat < n_lat - 1)

    def main_copy(k):
        return remote(
            apack.at[(lon + k) % n_lon], arecv.at[0, k], as_sem.at[0, k], ar_sem.at[0, k], device(0, k, ch)
        )

    def forward_copy(k):
        return remote(
            arecv.at[0, k] if k else apack.at[lon], arecv.at[1, k],
            as_sem.at[1, k], ar_sem.at[1, k], device(0, 0, near),
        )

    def band_copy(g):
        place = pl.ds(*bands[g][1:])
        return remote(bpack.at[place], brecv.at[place], bs_sem.at[g], br_sem.at[g], device(0, 0, near))

    def edge_copy(conv, side, p):
        return remote(
            epack.at[conv, side], erecv.at[conv, side, p], es_sem.at[conv, side, p], er_sem.at[conv, side, p],
            device((1, -1)[side] % n_lat, 0, (ch, near)[p]),
        )

    def piece_of(conv, g):
        return pl.ds(*(bands, blocks)[conv][g][1:])

    def far_copy(conv, g, k):
        src, dst = ((ysend1, yrecv1), (ysend2, yrecv2))[conv]
        slot, piece = (lon + k) % n_lon, piece_of(conv, g)
        return remote(
            src.at[slot, piece], dst.at[slot, piece],
            ys_sem.at[conv, g, k], yr_sem.at[conv, g, k], device(0, 0, far),
        )

    def along_copy(conv, g, k):
        src, dst = ((zsend1, zrecv1), (zsend2, zrecv2))[conv]
        piece = piece_of(conv, g)
        return remote(
            src.at[k, piece], dst.at[k, piece],
            zs_sem.at[conv, g, k], zr_sem.at[conv, g, k], device(0, k, ch),
        )

    def first_row(conv, g):
        ahead, behind = counts[conv]
        return jnp.where(flip, (behind, 0)[g], (0, ahead)[g])

    def lanes(p):
        return slice(p * part, (p + 1) * part)

    inside = slice(EDGE, EDGE + all_cols)

    def send_edge(conv, side, edge, due=True):
        @pl.when(jnp.logical_and(sends[side], due))
        def _():
            epack[conv, side] = edge.astype(bf16)
            for p in (1, 0):
                edge_copy(conv, side, p).start()

    def close(conv, g):
        for side in (0, 1):
            due = jnp.logical_not(flip) if side == g else flip
            row, inner = ((0, 1), (rows + 1, rows))[side]

            @pl.when(jnp.logical_and(gets[side], due))
            def _():
                for p in (0, 1):
                    edge_copy(conv, side, p).wait_recv()
                    field[row, inside, lanes(p)] = erecv[conv, side, p].astype(f32)

            @pl.when(jnp.logical_and(jnp.logical_not(gets[side]), due))
            def _():
                turn = all_cols // 2
                field[row, EDGE:EDGE + turn] = field[inner, EDGE + turn:EDGE + all_cols]
                field[row, EDGE + turn:EDGE + all_cols] = field[inner, EDGE:EDGE + turn]

        ahead = counts[conv][0] + 2
        behind = rows + 2 - ahead
        here = pl.ds(jnp.where(flip, (behind, 0)[g], (0, ahead)[g]), (ahead, behind)[g])
        field[here, EDGE - 1:EDGE] = field[here, EDGE + all_cols - 1:EDGE + all_cols]
        field[here, EDGE + all_cols:EDGE + all_cols + 1] = field[here, EDGE:EDGE + 1]
        for e in range(3):
            taps[here, :, e * 2 * part:(e + 1) * 2 * part] = field[
                here, EDGE - 1 + e:EDGE - 1 + e + all_cols
            ].astype(bf16)

    def exchange_one():
        for k in away:
            main_copy(k).start()
        forward_copy(0).start()

    def assemble_one():
        def place(k):
            return pl.ds(pl.multiple_of(EDGE + ((lon - k + n_lon) % n_lon) * cols, 8), cols)

        def cell_block(block):
            return unpack(block.astype(f32), cells).reshape(rows, cols, part)

        field[1:rows + 1, place(0), lanes(0)] = cell_block(apack[lon])
        for k in away:
            main_copy(k).wait_recv()
            forward_copy(k).start()
            field[1:rows + 1, place(k), lanes(0)] = cell_block(arecv[0, k])
        weights[0, 0][1].start()
        for side in (0, 1):
            send_edge(0, side, field[(rows, 1)[side], inside, lanes(0)])
        for k in [0] + away:
            forward_copy(k).wait_recv()
            field[1:rows + 1, place(k), lanes(1)] = cell_block(arecv[1, k])

    def hand_on(g, act):
        count, offset, size = bands[g]
        bpack[offset:offset + size] = act.astype(bf16)
        band_copy(g).start()
        band = unpack(act, count * all_cols)
        for side in (0, 1):
            turned = flip if side == g else jnp.logical_not(flip)
            send_edge(1, side, (band[-all_cols:], band[:all_cols])[side], turned)
        field[pl.ds(first_row(0, g) + 1, count), inside, lanes(0)] = band.reshape(count, all_cols, part)

    def assemble_two(g):
        count, offset, size = bands[g]
        band_copy(g).wait_recv()
        other = unpack(brecv[offset:offset + size].astype(f32), count * all_cols)
        field[pl.ds(first_row(0, g) + 1, count), inside, lanes(1)] = other.reshape(count, all_cols, part)
        close(1, g)

    def weights_here(conv, slot):
        local, other = weights[conv, slot]
        local.wait()
        other.wait_recv()

    def multiply(conv, slot, g):
        first, count = first_row(conv, g), counts[conv][g]
        total = None
        for a in range(3):
            term = jnp.dot(
                taps[pl.ds(first + a, count)].reshape(count * all_cols, 6 * part),
                w[conv, slot, a].reshape(6 * part, width),
                preferred_element_type=f32,
            )
            total = term if total is None else total + term
        return total

    inputs[0].wait()
    act = silu(x_vmem[0].astype(f32).reshape(cells, width))
    for j in range(n_lon):
        apack[j] = pack(act[:, lanes(j)], half).astype(bf16)
    pl.semaphore_wait(barrier, greeted)
    weights[0, 1][1].start()
    exchange_one()
    assemble_one()

    for g, (_, offset, size) in enumerate(bands):
        close(0, g)
        if g == 0:
            weights_here(0, 1)
        total = multiply(0, 1, g)
        for j in range(n_lon):
            ysend1[j, offset:offset + size] = pack(total[:, lanes(j)], size).astype(bf16)
        for k in order:
            far_copy(0, g, k).start()
    weights_here(0, 0)
    for g, (_, offset, size) in enumerate(bands):
        total = multiply(0, 0, g)
        for j in range(n_lon):
            own[j, offset:offset + size] = pack(total[:, lanes(j)], size)
    for slot in (1, 0):
        weights[1, slot][1].start()
    for g, (_, offset, size) in enumerate(bands):
        for k in order:
            far_copy(0, g, k).wait_recv()
            slot = (lon + k) % n_lon
            value = own[slot, offset:offset + size] + yrecv1[slot, offset:offset + size].astype(f32)
            if k:
                zsend1[k, offset:offset + size] = value.astype(bf16)
                along_copy(0, g, k).start()
            else:
                kept[offset:offset + size] = value
    for copy in inputs[1:]:
        copy.wait()
    bias = b1_vmem[:, lanes(0)]
    for j in away:
        bias = jnp.where(lon == j, b1_vmem[:, lanes(j)], bias)
    bias = jnp.concatenate([bias, bias], axis=1)

    def chunk(slot, g, k):
        count = counts[1][g]
        start = pl.multiple_of(((lon + k) % n_lon) * cols, 8)
        return acc[slot, pl.ds(first_row(1, g), count), pl.ds(start, cols), :].reshape(count * cols, width)

    def padded(value, size):
        if size > value.shape[0]:
            value = jnp.concatenate([value, jnp.zeros((size - value.shape[0], width), f32)], axis=0)
        return value.astype(bf16)

    def multiply_two(slot, g):
        count, offset, size = blocks[g]
        acc[slot, pl.ds(first_row(1, g), count)] = multiply(1, slot, g).reshape(count, all_cols, width)
        if slot:
            for k in order:
                ysend2[(lon + k) % n_lon, offset:offset + size] = padded(chunk(1, g, k), size)
                far_copy(1, g, k).start()

    def gather_one(g):
        _, offset, size = bands[g]
        hidden = kept[offset:offset + size]
        for k in away:
            along_copy(0, g, k).wait_recv()
            hidden = hidden + zrecv1[k, offset:offset + size].astype(f32)
        hand_on(g, silu(hidden + bias))

    def scatter_two(g, steps):
        count, offset, size = blocks[g]
        for k in steps:
            far_copy(1, g, k).wait_recv()
            other = yrecv2[(lon + k) % n_lon, offset:offset + size].astype(f32)
            value = chunk(0, g, k) + other[:count * cols]
            if k:
                zsend2[k, offset:offset + size] = padded(value, size)
                along_copy(1, g, k).start()
            else:
                out_ref[0, pl.ds(first_row(1, g), count)] = (value + b2_vmem[...]).reshape(count, cols, width)

    gather_one(0)
    assemble_two(0)
    weights_here(1, 1)
    multiply_two(1, 0)
    weights_here(1, 0)
    multiply_two(0, 0)
    gather_one(1)
    scatter_two(0, away)
    assemble_two(1)
    multiply_two(1, 1)
    scatter_two(0, [0])
    multiply_two(0, 1)
    scatter_two(1, order)
    for g, (count, offset, size) in enumerate(blocks):
        here = pl.ds(first_row(1, g), count)
        second = out_ref[0, here].reshape(count * cols, width)
        for k in away:
            along_copy(1, g, k).wait_recv()
            second = second + zrecv2[k, offset:offset + size].astype(f32)[:count * cols]
        out_ref[0, here] = second.reshape(count, cols, width)

    for k in order:
        forward_copy(k).wait_send()
        if k:
            main_copy(k).wait_send()
    for g in (0, 1):
        band_copy(g).wait_send()
    for conv in (0, 1):
        for side in (0, 1):
            @pl.when(sends[side])
            def _():
                for p in (0, 1):
                    edge_copy(conv, side, p).wait_send()
    for conv in (0, 1):
        for slot in (0, 1):
            weights[conv, slot][1].wait_send()
        for g in (0, 1):
            for k in order:
                far_copy(conv, g, k).wait_send()
                if k:
                    along_copy(conv, g, k).wait_send()


def body(n_lat, n_lon, features, kernel_one, bias_one, kernel_two, bias_two):
    _, rows, cols, width = features.shape
    cells, part, all_cols = rows * cols, width // n_lon, cols * n_lon
    half = round_up(-(-cells // 2), 16)
    counts = row_counts(rows)
    band_half, tall = row_groups(counts[0], all_cols, 2)[1], row_groups(counts[1], cols, 1)[1]
    bf16, f32 = jnp.bfloat16, jnp.float32
    dma = pltpu.SemaphoreType.DMA
    vmem = pl.BlockSpec(memory_space=pltpu.VMEM)
    anywhere = pl.BlockSpec(memory_space=pl.ANY)
    scratch = [
        pltpu.VMEM(features.shape, bf16),
        pltpu.VMEM((1, width), f32),
        pltpu.VMEM((1, width), f32),
        pltpu.VMEM((2, 2, 3, 3, 2, part, width), bf16),
        pltpu.VMEM((n_lon, half, 2 * part), bf16),
        pltpu.VMEM((2, n_lon, half, 2 * part), bf16),
        pltpu.VMEM((band_half, 2 * part), bf16),
        pltpu.VMEM((band_half, 2 * part), bf16),
        pltpu.VMEM((2, 2, all_cols, part), bf16),
        pltpu.VMEM((2, 2, 2, all_cols, part), bf16),
        pltpu.VMEM((rows + 2, all_cols + 2 * EDGE, 2 * part), f32),
        pltpu.VMEM((rows + 2, all_cols, 6 * part), bf16),
        pltpu.VMEM((n_lon, band_half, 2 * part), f32),
        pltpu.VMEM((band_half, 2 * part), f32),
        pltpu.VMEM((n_lon, band_half, 2 * part), bf16),
        pltpu.VMEM((n_lon, band_half, 2 * part), bf16),
        pltpu.VMEM((n_lon, band_half, 2 * part), bf16),
        pltpu.VMEM((n_lon, band_half, 2 * part), bf16),
        pltpu.VMEM((2, rows, all_cols, width), f32),
        pltpu.VMEM((n_lon, tall, width), bf16),
        pltpu.VMEM((n_lon, tall, width), bf16),
        pltpu.VMEM((n_lon, tall, width), bf16),
        pltpu.VMEM((n_lon, tall, width), bf16),
        dma((3,)), dma((2, 2)), dma((2, 2)), dma((2, 2)),
        dma((2, n_lon)), dma((2, n_lon)),
        dma((2,)), dma((2,)), dma((2, 2, 2)), dma((2, 2, 2)),
        dma((2, 2, n_lon)), dma((2, 2, n_lon)), dma((2, 2, n_lon)), dma((2, 2, n_lon)),
    ]
    second = pl.pallas_call(
        functools.partial(block_kernel, n_lat, n_lon),
        out_shape=jax.ShapeDtypeStruct(features.shape, f32),
        in_specs=[anywhere] * 5,
        out_specs=vmem,
        scratch_shapes=scratch,
        compiler_params=pltpu.CompilerParams(
            collective_id=0, has_side_effects=True, vmem_limit_bytes=56 * 2**20
        ),
        name="residual_block",
    )(features, kernel_one, bias_one.reshape(1, width), kernel_two, bias_two.reshape(1, width))
    return ((features.astype(f32) + second) * skip_scale).astype(bf16)


def solution(mesh):
    placed = (
        P(None, "lat", "lon", "ch"),
        P(None, None, "ch", "lon", None),
        P("ch"),
        P(None, None, "ch", "lon", None),
        P("ch"),
    )
    return jax.shard_map(
        functools.partial(body, mesh.shape["lat"], mesh.shape["lon"]),
        mesh=mesh, in_specs=placed, out_specs=P(None, "lat", "lon", "ch"), check_vma=False,
    )
```

```python
import functools

import jax
import jax.numpy as jnp
from jax import lax
from jax.experimental import pallas as pl
from jax.experimental.pallas import tpu as pltpu
from jax.sharding import PartitionSpec as P

skip_scale = 0.7071067811865476
MESH = pl.DeviceIdType.MESH
EDGE = 8


def round_up(value, step):
    return -(-value // step) * step


def silu(value):
    return value / (1.0 + jnp.exp(-value))


def pack(value, half):
    count, part = value.shape
    lower = value[half:]
    if 2 * half > count:
        lower = jnp.concatenate([lower, jnp.zeros((2 * half - count, part), value.dtype)], axis=0)
    return jnp.concatenate([value[:half], lower], axis=1)


def unpack(block, count):
    half, part = block.shape[0], block.shape[1] // 2
    return jnp.concatenate([block[:, :part], block[:count - half, part:]], axis=0)


def row_groups(counts, per_row, packed):
    groups, offset = [], 0
    for count in counts:
        size = round_up(-(-count * per_row // packed), 16)
        groups.append((count, offset, size))
        offset += size
    return groups, offset


def row_counts(rows):
    ahead = -(-rows // 2)
    return (ahead, rows - ahead), (ahead - 1, rows - ahead + 1)


def block_kernel(
    n_lat, n_lon, x_ref, k1_ref, b1_ref, k2_ref, b2_ref, out_ref,
    x_vmem, b1_vmem, b2_vmem, w, apack, arecv, bpack, brecv, epack, erecv, field, taps,
    own, kept, ysend1, yrecv1, zsend1, zrecv1, acc, ysend2, yrecv2, zsend2, zrecv2,
    in_sem, wl_sem, ws_sem, wr_sem, as_sem, ar_sem,
    bs_sem, br_sem, es_sem, er_sem, ys_sem, yr_sem, zs_sem, zr_sem,
):
    rows, cols, width = x_ref.shape[1:]
    cells = rows * cols
    part = width // n_lon
    half = apack.shape[1]
    all_cols = cols * n_lon
    counts = row_counts(rows)
    bands = row_groups(counts[0], all_cols, 2)[0]
    blocks = row_groups(counts[1], cols, 1)[0]
    f32, bf16 = jnp.float32, jnp.bfloat16
    lat, lon, ch = lax.axis_index("lat"), lax.axis_index("lon"), lax.axis_index("ch")
    flip = lat >= n_lat - n_lat // 2
    near = ch + 1 - 2 * (ch % 2)
    far = ch + 2 - 4 * ((ch // 2) % 2)
    near_far = near + 2 - 4 * ((near // 2) % 2)
    away = sorted(range(1, n_lon), key=lambda k: abs(2 * k - n_lon))
    order = away + [0]

    def device(up, along, channel):
        return {"lat": (lat + up) % n_lat, "lon": (lon + along) % n_lon, "ch": channel}

    def remote(src, dst, send, recv, target):
        return pltpu.make_async_remote_copy(
            src_ref=src, dst_ref=dst, send_sem=send, recv_sem=recv,
            device_id=target, device_id_type=MESH,
        )

    def weight_copies(conv, slot):
        source = (k1_ref, k2_ref)[conv]
        mine, theirs = ((ch, near), (far, near_far))[slot]

        def outputs(group):
            return source.at[:, :, 0, :, pl.ds(pl.multiple_of(group * width, width), width)]

        return (
            pltpu.make_async_copy(outputs(mine), w.at[conv, slot, :, :, 0], wl_sem.at[conv, slot]),
            remote(
                outputs(theirs), w.at[conv, slot, :, :, 1],
                ws_sem.at[conv, slot], wr_sem.at[conv, slot], device(0, 0, near),
            ),
        )

    barrier = pltpu.get_barrier_semaphore()
    greeted = 0
    peers = [(0, along, ch) for along in away] + [(0, 0, near), (0, 0, far)]
    peers += [(up, 0, channel) for up in sorted({1, n_lat - 1}) for channel in (ch, near)]
    for peer in peers:
        pl.semaphore_signal(barrier, inc=1, device_id=device(*peer), device_id_type=MESH)
        greeted += 1

    inputs = [
        pltpu.make_async_copy(src, dst, in_sem.at[i])
        for i, (src, dst) in enumerate(((x_ref, x_vmem), (b1_ref, b1_vmem), (b2_ref, b2_vmem)))
    ]
    for copy in inputs:
        copy.start()
    weights = {(conv, slot): weight_copies(conv, slot) for conv in (0, 1) for slot in (1, 0)}
    for local, _ in weights.values():
        local.start()

    sends = (lat < n_lat - 1, lat > 0)
    gets = (lat > 0, lat < n_lat - 1)

    def main_copy(k):
        return remote(
            apack.at[(lon + k) % n_lon], arecv.at[0, k], as_sem.at[0, k], ar_sem.at[0, k], device(0, k, ch)
        )

    def forward_copy(k):
        return remote(
            arecv.at[0, k] if k else apack.at[lon], arecv.at[1, k],
            as_sem.at[1, k], ar_sem.at[1, k], device(0, 0, near),
        )

    def band_copy(g):
        place = pl.ds(*bands[g][1:])
        return remote(bpack.at[place], brecv.at[place], bs_sem.at[g], br_sem.at[g], device(0, 0, near))

    def edge_copy(conv, side, p):
        return remote(
            epack.at[conv, side], erecv.at[conv, side, p], es_sem.at[conv, side, p], er_sem.at[conv, side, p],
            device((1, -1)[side] % n_lat, 0, (ch, near)[p]),
        )

    def piece_of(conv, g):
        return pl.ds(*(bands, blocks)[conv][g][1:])

    def far_copy(conv, g, k):
        src, dst = ((ysend1, yrecv1), (ysend2, yrecv2))[conv]
        slot, piece = (lon + k) % n_lon, piece_of(conv, g)
        return remote(
            src.at[slot, piece], dst.at[slot, piece],
            ys_sem.at[conv, g, k], yr_sem.at[conv, g, k], device(0, 0, far),
        )

    def along_copy(conv, g, k):
        src, dst = ((zsend1, zrecv1), (zsend2, zrecv2))[conv]
        piece = piece_of(conv, g)
        return remote(
            src.at[k, piece], dst.at[k, piece],
            zs_sem.at[conv, g, k], zr_sem.at[conv, g, k], device(0, k, ch),
        )

    def first_row(conv, g):
        ahead, behind = counts[conv]
        return jnp.where(flip, (behind, 0)[g], (0, ahead)[g])

    def lanes(p):
        return slice(p * part, (p + 1) * part)

    inside = slice(EDGE, EDGE + all_cols)

    def send_edge(conv, side, edge, due=True):
        @pl.when(jnp.logical_and(sends[side], due))
        def _():
            epack[conv, side] = edge.astype(bf16)
            for p in (1, 0):
                edge_copy(conv, side, p).start()

    def close(conv, g):
        for side in (0, 1):
            due = jnp.logical_not(flip) if side == g else flip
            row, inner = ((0, 1), (rows + 1, rows))[side]

            @pl.when(jnp.logical_and(gets[side], due))
            def _():
                for p in (0, 1):
                    edge_copy(conv, side, p).wait_recv()
                    field[row, inside, lanes(p)] = erecv[conv, side, p].astype(f32)

            @pl.when(jnp.logical_and(jnp.logical_not(gets[side]), due))
            def _():
                turn = all_cols // 2
                field[row, EDGE:EDGE + turn] = field[inner, EDGE + turn:EDGE + all_cols]
                field[row, EDGE + turn:EDGE + all_cols] = field[inner, EDGE:EDGE + turn]

        ahead = counts[conv][0] + 2
        behind = rows + 2 - ahead
        here = pl.ds(jnp.where(flip, (behind, 0)[g], (0, ahead)[g]), (ahead, behind)[g])
        field[here, EDGE - 1:EDGE] = field[here, EDGE + all_cols - 1:EDGE + all_cols]
        field[here, EDGE + all_cols:EDGE + all_cols + 1] = field[here, EDGE:EDGE + 1]
        for e in range(3):
            taps[here, :, e * 2 * part:(e + 1) * 2 * part] = field[
                here, EDGE - 1 + e:EDGE - 1 + e + all_cols
            ].astype(bf16)

    def exchange_one():
        for k in away:
            main_copy(k).start()
        forward_copy(0).start()

    def assemble_one():
        def place(k):
            return pl.ds(pl.multiple_of(EDGE + ((lon - k + n_lon) % n_lon) * cols, 8), cols)

        def cell_block(block):
            return unpack(block.astype(f32), cells).reshape(rows, cols, part)

        field[1:rows + 1, place(0), lanes(0)] = cell_block(apack[lon])
        for k in away:
            main_copy(k).wait_recv()
            forward_copy(k).start()
            field[1:rows + 1, place(k), lanes(0)] = cell_block(arecv[0, k])
        weights[0, 0][1].start()
        for side in (0, 1):
            send_edge(0, side, field[(rows, 1)[side], inside, lanes(0)])
        for k in [0] + away:
            forward_copy(k).wait_recv()
            field[1:rows + 1, place(k), lanes(1)] = cell_block(arecv[1, k])

    def hand_on(g, act):
        count, offset, size = bands[g]
        bpack[offset:offset + size] = act.astype(bf16)
        band_copy(g).start()
        band = unpack(act, count * all_cols)
        for side in (0, 1):
            turned = flip if side == g else jnp.logical_not(flip)
            send_edge(1, side, (band[-all_cols:], band[:all_cols])[side], turned)
        field[pl.ds(first_row(0, g) + 1, count), inside, lanes(0)] = band.reshape(count, all_cols, part)

    def assemble_two(g):
        count, offset, size = bands[g]
        band_copy(g).wait_recv()
        other = unpack(brecv[offset:offset + size].astype(f32), count * all_cols)
        field[pl.ds(first_row(0, g) + 1, count), inside, lanes(1)] = other.reshape(count, all_cols, part)
        close(1, g)

    def weights_here(conv, slot):
        local, other = weights[conv, slot]
        local.wait()
        other.wait_recv()

    def multiply(conv, slot, g):
        first, count = first_row(conv, g), counts[conv][g]
        total = None
        for a in range(3):
            term = jnp.dot(
                taps[pl.ds(first + a, count)].reshape(count * all_cols, 6 * part),
                w[conv, slot, a].reshape(6 * part, width),
                preferred_element_type=f32,
            )
            total = term if total is None else total + term
        return total

    inputs[0].wait()
    act = silu(x_vmem[0].astype(f32).reshape(cells, width))
    for j in range(n_lon):
        apack[j] = pack(act[:, lanes(j)], half).astype(bf16)
    pl.semaphore_wait(barrier, greeted)
    weights[0, 1][1].start()
    exchange_one()
    assemble_one()

    for g, (_, offset, size) in enumerate(bands):
        close(0, g)
        if g == 0:
            weights_here(0, 1)
        total = multiply(0, 1, g)
        for j in range(n_lon):
            ysend1[j, offset:offset + size] = pack(total[:, lanes(j)], size).astype(bf16)
        for k in order:
            far_copy(0, g, k).start()
    weights_here(0, 0)
    for g, (_, offset, size) in enumerate(bands):
        total = multiply(0, 0, g)
        for j in range(n_lon):
            own[j, offset:offset + size] = pack(total[:, lanes(j)], size)
        for k in order:
            far_copy(0, g, k).wait_recv()
            slot = (lon + k) % n_lon
            value = own[slot, offset:offset + size] + yrecv1[slot, offset:offset + size].astype(f32)
            if k:
                zsend1[k, offset:offset + size] = value.astype(bf16)
                along_copy(0, g, k).start()
            else:
                kept[offset:offset + size] = value
    for slot in (1, 0):
        weights[1, slot][1].start()
    for copy in inputs[1:]:
        copy.wait()
    bias = b1_vmem[:, lanes(0)]
    for j in away:
        bias = jnp.where(lon == j, b1_vmem[:, lanes(j)], bias)
    bias = jnp.concatenate([bias, bias], axis=1)

    def chunk(slot, g, k):
        count = counts[1][g]
        start = pl.multiple_of(((lon + k) % n_lon) * cols, 8)
        return acc[slot, pl.ds(first_row(1, g), count), pl.ds(start, cols), :].reshape(count * cols, width)

    def padded(value, size):
        if size > value.shape[0]:
            value = jnp.concatenate([value, jnp.zeros((size - value.shape[0], width), f32)], axis=0)
        return value.astype(bf16)

    def multiply_two(slot, g):
        count, offset, size = blocks[g]
        acc[slot, pl.ds(first_row(1, g), count)] = multiply(1, slot, g).reshape(count, all_cols, width)
        if slot:
            for k in order:
                ysend2[(lon + k) % n_lon, offset:offset + size] = padded(chunk(1, g, k), size)
                far_copy(1, g, k).start()

    def gather_one(g):
        _, offset, size = bands[g]
        hidden = kept[offset:offset + size]
        for k in away:
            along_copy(0, g, k).wait_recv()
            hidden = hidden + zrecv1[k, offset:offset + size].astype(f32)
        hand_on(g, silu(hidden + bias))

    def scatter_two(g):
        count, offset, size = blocks[g]
        for k in order:
            far_copy(1, g, k).wait_recv()
            other = yrecv2[(lon + k) % n_lon, offset:offset + size].astype(f32)
            value = chunk(0, g, k) + other[:count * cols]
            if k:
                zsend2[k, offset:offset + size] = padded(value, size)
                along_copy(1, g, k).start()
            else:
                out_ref[0, pl.ds(first_row(1, g), count)] = (value + b2_vmem[...]).reshape(count, cols, width)

    gather_one(0)
    assemble_two(0)
    weights_here(1, 1)
    multiply_two(1, 0)
    gather_one(1)
    weights_here(1, 0)
    multiply_two(0, 0)
    assemble_two(1)
    multiply_two(1, 1)
    scatter_two(0)
    multiply_two(0, 1)
    scatter_two(1)
    for g, (count, offset, size) in enumerate(blocks):
        here = pl.ds(first_row(1, g), count)
        second = out_ref[0, here].reshape(count * cols, width)
        for k in away:
            along_copy(1, g, k).wait_recv()
            second = second + zrecv2[k, offset:offset + size].astype(f32)[:count * cols]
        out_ref[0, here] = second.reshape(count, cols, width)

    for k in order:
        forward_copy(k).wait_send()
        if k:
            main_copy(k).wait_send()
    for g in (0, 1):
        band_copy(g).wait_send()
    for conv in (0, 1):
        for side in (0, 1):
            @pl.when(sends[side])
            def _():
                for p in (0, 1):
                    edge_copy(conv, side, p).wait_send()
    for conv in (0, 1):
        for slot in (0, 1):
            weights[conv, slot][1].wait_send()
        for g in (0, 1):
            for k in order:
                far_copy(conv, g, k).wait_send()
                if k:
                    along_copy(conv, g, k).wait_send()


def body(n_lat, n_lon, features, kernel_one, bias_one, kernel_two, bias_two):
    _, rows, cols, width = features.shape
    cells, part, all_cols = rows * cols, width // n_lon, cols * n_lon
    half = round_up(-(-cells // 2), 16)
    counts = row_counts(rows)
    band_half, tall = row_groups(counts[0], all_cols, 2)[1], row_groups(counts[1], cols, 1)[1]
    bf16, f32 = jnp.bfloat16, jnp.float32
    dma = pltpu.SemaphoreType.DMA
    vmem = pl.BlockSpec(memory_space=pltpu.VMEM)
    anywhere = pl.BlockSpec(memory_space=pl.ANY)
    second = pl.pallas_call(
        functools.partial(block_kernel, n_lat, n_lon),
        out_shape=jax.ShapeDtypeStruct(features.shape, f32),
        in_specs=[anywhere] * 5,
        out_specs=vmem,
        scratch_shapes=[
            pltpu.VMEM(features.shape, bf16),
            pltpu.VMEM((1, width), f32),
            pltpu.VMEM((1, width), f32),
            pltpu.VMEM((2, 2, 3, 3, 2, part, width), bf16),
            pltpu.VMEM((n_lon, half, 2 * part), bf16),
            pltpu.VMEM((2, n_lon, half, 2 * part), bf16),
            pltpu.VMEM((band_half, 2 * part), bf16),
            pltpu.VMEM((band_half, 2 * part), bf16),
            pltpu.VMEM((2, 2, all_cols, part), bf16),
            pltpu.VMEM((2, 2, 2, all_cols, part), bf16),
            pltpu.VMEM((rows + 2, all_cols + 2 * EDGE, 2 * part), f32),
            pltpu.VMEM((rows + 2, all_cols, 6 * part), bf16),
            pltpu.VMEM((n_lon, band_half, 2 * part), f32),
            pltpu.VMEM((band_half, 2 * part), f32),
            pltpu.VMEM((n_lon, band_half, 2 * part), bf16),
            pltpu.VMEM((n_lon, band_half, 2 * part), bf16),
            pltpu.VMEM((n_lon, band_half, 2 * part), bf16),
            pltpu.VMEM((n_lon, band_half, 2 * part), bf16),
            pltpu.VMEM((2, rows, all_cols, width), f32),
            pltpu.VMEM((n_lon, tall, width), bf16),
            pltpu.VMEM((n_lon, tall, width), bf16),
            pltpu.VMEM((n_lon, tall, width), bf16),
            pltpu.VMEM((n_lon, tall, width), bf16),
            dma((3,)), dma((2, 2)), dma((2, 2)), dma((2, 2)),
            dma((2, n_lon)), dma((2, n_lon)),
            dma((2,)), dma((2,)), dma((2, 2, 2)), dma((2, 2, 2)),
            dma((2, 2, n_lon)), dma((2, 2, n_lon)), dma((2, 2, n_lon)), dma((2, 2, n_lon)),
        ],
        compiler_params=pltpu.CompilerParams(
            collective_id=0, has_side_effects=True, vmem_limit_bytes=56 * 2**20
        ),
        name="residual_block",
    )(features, kernel_one, bias_one.reshape(1, width), kernel_two, bias_two.reshape(1, width))
    return ((features.astype(f32) + second) * skip_scale).astype(bf16)


def solution(mesh):
    placed = (
        P(None, "lat", "lon", "ch"),
        P(None, None, "ch", "lon", None),
        P("ch"),
        P(None, None, "ch", "lon", None),
        P("ch"),
    )
    return jax.shard_map(
        functools.partial(body, mesh.shape["lat"], mesh.shape["lon"]),
        mesh=mesh, in_specs=placed, out_specs=P(None, "lat", "lon", "ch"), check_vma=False,
    )
```
